256 devices in a mesh: grp: 4 (over y_hi, core), uly: 8 (over z), ctx: 8 (over y_lo, x).
Axes of the slice: x: 4, y: 4 (y_hi: 2, y_lo: 2; y = y_hi * 2 + y_lo), z: 8, core: 2. Of those that a mesh axis runs over, the one named last changes fastest.
Arguments:
- queries: bfloat16 [32768, 4096], P(('grp', 'uly', 'ctx')), may hold values from -80 to 80
- keys_in: bfloat16 [32768, 1024], P(('grp', 'uly', 'ctx')), may hold values from -6 to 6
- values_in: bfloat16 [32768, 1024], P(('grp', 'uly', 'ctx')), may hold values from -6 to 6
- out_grad: bfloat16 [32768, 4096], P(('grp', 'uly', 'ctx')), may hold values from -6 to 6
- lengths: int32 [4, 2, 3], P('grp'), may hold values from 1 to 2048, 4096 in all within a row
- prompt_keys: bfloat16 [128, 1024], P(('grp', 'ctx'), 'uly'), may hold values from -6 to 6
- prompt_values: bfloat16 [128, 1024], P(('grp', 'ctx'), 'uly'), may hold values from -6 to 6
Outputs:
- attention_output: bfloat16 [32768, 4096], P(('grp', 'uly', 'ctx'))
- query_gradient: bfloat16 [32768, 4096], P(('grp', 'uly', 'ctx'))
- response_key_grad: bfloat16 [32768, 1024], P(('grp', 'uly', 'ctx'))
- response_value_grad: bfloat16 [32768, 1024], P(('grp', 'uly', 'ctx'))
- prompt_key_grad: bfloat16 [128, 1024], P(('grp', 'ctx'), 'uly')
- prompt_value_grad: bfloat16 [128, 1024], P(('grp', 'ctx'), 'uly')
The draws below stay inside these ranges and needn't reach their ends.
All inputs are finite; a program needn't handle non-finite values.
Results may differ from the reference program's by a relative error of at most 0.03.
The reference program's roundings to bfloat16 on the way (of `prob_half` and `score_grad`) count: a program that leaves them out, or rounds other values in their place, can miss the bound.
Values may be sent and summed in bfloat16 or wider, within the bound.
A program may use at most 128 MiB of HBM per device.

```python
import math
import jax
import jax.numpy as jnp
import numpy as np
from jax import lax

H = 32
KEY_VALUE_HEADS = 8
HEAD_WIDTH = 128
TOK_DEV = 128
PROMPT_TOKENS = 128
RUNS = 2
RESP = 3
SLICE = 4096
MOST = 2048
TOKENS = 32768
N_GRP = 4


def draw_queries(key, part):
    key = jax.random.fold_in(key, 17)
    base_key = jax.random.fold_in(key, 0)
    values = jnp.clip(jax.random.normal(base_key, (TOKENS, H, HEAD_WIDTH), jnp.float32), -6.5, 6.5)
    return values.reshape(TOKENS, H * HEAD_WIDTH).astype(jnp.bfloat16)


def steps_of(key, shape, shards, smallest, largest):
    gain = 1.0
    for axis_at, blocks in shards:
        heights = jax.random.uniform(jax.random.fold_in(jax.random.fold_in(key, 6), axis_at), (blocks,), jnp.float32, smallest / len(shards), largest / len(shards))
        gain = gain * jnp.repeat(jnp.exp(heights), shape[axis_at] // blocks).reshape((-1,) + (1,) * (len(shape) - 1 - axis_at))
    return gain


def split_up(count, total, most, slope):
    weights = [(1 << 20) // math.isqrt(grade ** slope) + 1 for grade in range(2, count + 1)]
    spare, holding = total - most - (count - 1), [1] * (count - 1)
    while spare > 0:
        movable = [i for i in range(count - 1) if holding[i] < most]
        whole, budget = sum([weights[i] for i in movable]), spare
        for i in movable:
            more = min(most - holding[i], max(1, budget * weights[i] // whole), spare)
            holding[i] = holding[i] + more
            spare = spare - more
    return np.array([most] + holding)


def ragged_sizes(rng, amount, total, limit, skew):
    if amount == 2:
        one = jax.random.randint(rng, (), max(1, total - limit), min(limit, total - 1) + 1)
        return jnp.stack([one, total - one])
    sizes = jnp.asarray(split_up(amount, total, limit, skew), jnp.int32)
    pairs = (amount - 1) // 2
    giver, receiver = sizes[1:1 + 2 * pairs:2], sizes[2:2 + 2 * pairs:2]
    margin = jnp.minimum(giver - 1, limit - receiver)
    shifted = jax.random.randint(jax.random.fold_in(rng, 1), (pairs,), 0, 1 << 20) % (margin + 1)
    sizes = sizes.at[1:1 + 2 * pairs:2].set(giver - shifted).at[2:2 + 2 * pairs:2].set(receiver + shifted)
    return sizes[jax.random.permutation(jax.random.fold_in(rng, 2), amount)]


def bell_draw(rng, shape, width, bound, pieces=(), held_as=jnp.bfloat16):
    array = width * jax.random.normal(rng, shape, jnp.float32)
    if pieces:
        array = array * steps_of(rng, shape, pieces, -0.22, 0.18)
    return jnp.clip(array, -bound, bound).astype(held_as)


def setup_inputs(seed: int = 0) -> dict:
    splits = jax.random.split(jax.random.key(seed), 8)
    queries = draw_queries(jax.random.fold_in(splits[7], 71), 0)
    keys_in = bell_draw(splits[1], (TOKENS, KEY_VALUE_HEADS * HEAD_WIDTH), 1.0, 6.0, ((0, 256),))
    values_in = bell_draw(splits[2], (TOKENS, KEY_VALUE_HEADS * HEAD_WIDTH), 1.0, 6.0, ((0, 256),))
    out_grad = bell_draw(splits[3], (TOKENS, H * HEAD_WIDTH), 1.0, 6.0, ((0, 256),))
    lengths = jax.vmap(lambda own: ragged_sizes(own, RESP, SLICE, MOST, 2))(jax.random.split(splits[4], N_GRP * RUNS)).reshape((N_GRP, RUNS, RESP)).astype(jnp.int32)
    prompt_keys = bell_draw(splits[5], (PROMPT_TOKENS, KEY_VALUE_HEADS * HEAD_WIDTH), 1.0, 6.0, ((0, 32), (1, 8)))
    prompt_values = bell_draw(splits[6], (PROMPT_TOKENS, KEY_VALUE_HEADS * HEAD_WIDTH), 1.0, 6.0, ((0, 32), (1, 8)))
    return dict(queries=queries, keys_in=keys_in, values_in=values_in, out_grad=out_grad, lengths=lengths, prompt_keys=prompt_keys, prompt_values=prompt_values)


theta_base = 1000000.0
neg_fill = -1.0e30


def rounded(values):
    return lax.optimization_barrier(values.astype(jnp.bfloat16))


def rotate_rows(values, positions, direction):
    count = values.shape[0]
    half_dim = HEAD_WIDTH // 2
    shaped = values.astype(jnp.float32).reshape(count, -1, HEAD_WIDTH)
    frequency = jnp.exp(-(2.0 * jnp.arange(half_dim, dtype=jnp.float32) / HEAD_WIDTH) * jnp.log(jnp.float32(theta_base)))
    angles = positions.astype(jnp.float32)[:, None] * frequency[None, :]
    cosine = jnp.cos(angles)[:, None, :]
    sine_part = direction * jnp.sin(angles)[:, None, :]
    first_half = shaped[..., :half_dim]
    second_half = shaped[..., half_dim:]
    turned = jnp.concatenate([first_half * cosine - second_half * sine_part, second_half * cosine + first_half * sine_part], axis=-1)
    return turned.reshape(count, -1)


def segment_begins(length_row, count):
    segment_ends = jnp.cumsum(length_row.astype(jnp.int32))
    token_index = jnp.arange(count, dtype=jnp.int32)
    closed = (segment_ends[None, :] <= token_index[:, None]).astype(jnp.int32)
    return jnp.sum(length_row.astype(jnp.int32)[None, :] * closed, axis=1)


def group_begins(length_rows, run_len):
    run_count = length_rows.shape[0]
    starts = jax.vmap(lambda row: segment_begins(row, run_len))(length_rows)
    offsets = (jnp.arange(run_count, dtype=jnp.int32) * run_len)[:, None]
    return (starts + offsets).astype(jnp.int32).reshape(-1)


def attend_block(query_blk, grad_blk, keys_win, values_win, prompt_k, prompt_v, allowed):
    score_scale = HEAD_WIDTH ** -0.5
    key_block = jnp.concatenate([prompt_k, keys_win], axis=0).astype(jnp.float32)
    value_block = jnp.concatenate([prompt_v, values_win], axis=0).astype(jnp.float32)
    query_f32 = query_blk.astype(jnp.float32)
    grad_f32 = grad_blk.astype(jnp.float32)
    scores = jnp.einsum('qhgd,khd->hgqk', query_f32, key_block) * score_scale
    live_mask = jnp.concatenate([jnp.ones((allowed.shape[0], prompt_k.shape[0]), dtype=bool), allowed], axis=1)
    scores = jnp.where(live_mask[None, None], scores, neg_fill)
    row_top = jnp.max(scores, axis=-1, keepdims=True)
    powered = jnp.exp(scores - row_top)
    attn_prob = powered / jnp.sum(powered, axis=-1, keepdims=True)
    prob_half = rounded(attn_prob)
    output_full = jnp.einsum('hgqk,khd->qhgd', prob_half.astype(jnp.float32), value_block)
    output_halfway = rounded(output_full)
    row_delta = jnp.sum(grad_f32 * output_halfway.astype(jnp.float32), axis=-1)
    prob_grad = jnp.einsum('qhgd,khd->hgqk', grad_f32, value_block)
    score_grad = rounded(attn_prob * (prob_grad - jnp.transpose(row_delta, (1, 2, 0))[..., None]) * score_scale)
    query_piece = jnp.einsum('hgqk,khd->qhgd', score_grad.astype(jnp.float32), key_block)
    key_part = jnp.einsum('hgqk,qhgd->khd', score_grad.astype(jnp.float32), query_f32)
    value_part = jnp.einsum('hgqk,qhgd->khd', prob_half.astype(jnp.float32), grad_f32)
    prompt_length = prompt_k.shape[0]
    return output_halfway, query_piece, key_part[:prompt_length], key_part[prompt_length:], value_part[:prompt_length], value_part[prompt_length:]


def one_group(query_g, key_g, value_g, grad_g, length_rows, prompt_k, prompt_v):
    group_tokens = query_g.shape[0]
    block_len = TOK_DEV
    window = MOST + TOK_DEV
    group_size = H // KEY_VALUE_HEADS
    block_count = group_tokens // block_len
    begins = group_begins(length_rows, group_tokens // RUNS)
    token_index = jnp.arange(group_tokens, dtype=jnp.int32)
    positions = PROMPT_TOKENS + token_index - begins
    query_rot = rounded(rotate_rows(query_g, positions, 1.0))
    key_rot = rounded(rotate_rows(key_g, positions, 1.0))
    query_blocks = query_rot.reshape(block_count, block_len, KEY_VALUE_HEADS, group_size, HEAD_WIDTH)
    grad_blocks = grad_g.reshape(block_count, block_len, KEY_VALUE_HEADS, group_size, HEAD_WIDTH)
    key_three = key_rot.reshape(group_tokens, KEY_VALUE_HEADS, HEAD_WIDTH)
    value_three = value_g.reshape(group_tokens, KEY_VALUE_HEADS, HEAD_WIDTH)
    prompt_k3 = prompt_k.reshape(PROMPT_TOKENS, KEY_VALUE_HEADS, HEAD_WIDTH)
    prompt_v3 = prompt_v.reshape(PROMPT_TOKENS, KEY_VALUE_HEADS, HEAD_WIDTH)

    def step_block(carried_state, item):
        key_running_sum, value_running_sum, prompt_key_running, prompt_value_running = carried_state
        block_id, query_blk, grad_blk = item
        query_start = block_id * block_len
        window_start = jnp.maximum(query_start + block_len - window, 0).astype(jnp.int32)
        keys_win = lax.dynamic_slice_in_dim(key_three, window_start, window, 0)
        values_win = lax.dynamic_slice_in_dim(value_three, window_start, window, 0)
        query_pos = query_start + jnp.arange(block_len, dtype=jnp.int32)
        key_pos = window_start + jnp.arange(window, dtype=jnp.int32)
        begins_blk = lax.dynamic_slice_in_dim(begins, query_start, block_len, 0)
        allowed = (key_pos[None, :] >= begins_blk[:, None]) & (key_pos[None, :] <= query_pos[:, None])
        output_halfway, query_piece, prompt_key_piece, key_part, prompt_value_piece, value_part = attend_block(
            query_blk, grad_blk, keys_win, values_win, prompt_k3, prompt_v3, allowed)
        key_running_sum = lax.dynamic_update_slice_in_dim(key_running_sum, lax.dynamic_slice_in_dim(key_running_sum, window_start, window, 0) + key_part, window_start, 0)
        value_running_sum = lax.dynamic_update_slice_in_dim(value_running_sum, lax.dynamic_slice_in_dim(value_running_sum, window_start, window, 0) + value_part, window_start, 0)
        return (key_running_sum, value_running_sum, prompt_key_running + prompt_key_piece, prompt_value_running + prompt_value_piece), (output_halfway, query_piece)

    start_state = (jnp.zeros((group_tokens, KEY_VALUE_HEADS, HEAD_WIDTH), jnp.float32), jnp.zeros((group_tokens, KEY_VALUE_HEADS, HEAD_WIDTH), jnp.float32),
                   jnp.zeros((PROMPT_TOKENS, KEY_VALUE_HEADS, HEAD_WIDTH), jnp.float32), jnp.zeros((PROMPT_TOKENS, KEY_VALUE_HEADS, HEAD_WIDTH), jnp.float32))
    closing_state, stacked = lax.scan(step_block, start_state, (jnp.arange(block_count, dtype=jnp.int32), query_blocks, grad_blocks))
    key_running_sum, value_running_sum, prompt_key_running, prompt_value_running = closing_state
    output_halfway, query_piece = stacked
    attention_output = output_halfway.reshape(group_tokens, H * HEAD_WIDTH)
    query_gradient = rotate_rows(query_piece.reshape(group_tokens, H * HEAD_WIDTH), positions, -1.0).astype(jnp.bfloat16)
    response_key_grad = rotate_rows(key_running_sum.reshape(group_tokens, KEY_VALUE_HEADS * HEAD_WIDTH), positions, -1.0).astype(jnp.bfloat16)
    response_value_grad = value_running_sum.reshape(group_tokens, KEY_VALUE_HEADS * HEAD_WIDTH).astype(jnp.bfloat16)
    return attention_output, query_gradient, response_key_grad, response_value_grad, prompt_key_running.reshape(PROMPT_TOKENS, KEY_VALUE_HEADS * HEAD_WIDTH), prompt_value_running.reshape(PROMPT_TOKENS, KEY_VALUE_HEADS * HEAD_WIDTH)


def reference(queries, keys_in, values_in, out_grad, lengths, prompt_keys, prompt_values):
    group_tokens = queries.shape[0] // N_GRP
    outputs = []
    query_grads = []
    key_grads = []
    value_grads = []
    prompt_ksum = jnp.zeros((PROMPT_TOKENS, KEY_VALUE_HEADS * HEAD_WIDTH), jnp.float32)
    prompt_vsum = jnp.zeros((PROMPT_TOKENS, KEY_VALUE_HEADS * HEAD_WIDTH), jnp.float32)
    for group in range(N_GRP):
        lower = group * group_tokens
        upper = lower + group_tokens
        result = one_group(queries[lower:upper], keys_in[lower:upper], values_in[lower:upper],
                           out_grad[lower:upper], lengths[group], prompt_keys, prompt_values)
        outputs.append(result[0])
        query_grads.append(result[1])
        key_grads.append(result[2])
        value_grads.append(result[3])
        prompt_ksum = prompt_ksum + result[4]
        prompt_vsum = prompt_vsum + result[5]
    return (jnp.concatenate(outputs, axis=0), jnp.concatenate(query_grads, axis=0),
            jnp.concatenate(key_grads, axis=0), jnp.concatenate(value_grads, axis=0),
            prompt_ksum.astype(jnp.bfloat16), prompt_vsum.astype(jnp.bfloat16))
```

```python
import functools

import jax
import jax.numpy as jnp
import numpy as np
from jax import lax
from jax.experimental import pallas as pl
from jax.experimental.pallas import tpu as pltpu
from jax.sharding import PartitionSpec as P

H = 32
KEY_VALUE_HEADS = 8
HEAD_WIDTH = 128
PROMPT_TOKENS = 128
theta_base = 1000000.0
neg_fill = -1e30

N_GRP, N_ULY, N_CTX = 4, 8, 8
BLOCK = 128
CHUNK = N_CTX * BLOCK
RUN_PLACES = 4
RESP = 3
QH = H // KEY_VALUE_HEADS
WIN = 3 * CHUNK
TK = 256
TQ = 256
LANES = QH * TQ
SCALE = HEAD_WIDTH**-0.5
C2 = SCALE * 1.4426950408889634
MESH = pl.DeviceIdType.MESH
f32, bf16 = jnp.float32, jnp.bfloat16


def frequencies():
    half = np.exp(-(2.0 * np.arange(64) / HEAD_WIDTH) * np.log(theta_base)).astype(np.float32)
    return np.concatenate([half, half])


def begins_of(tau, len_ref, run):
    l0, l1 = len_ref[run, 0], len_ref[run, 1]
    l2 = len_ref[run, 2]
    e1 = l0 + l1
    zero = jnp.zeros_like(tau)
    return (
        jnp.where(tau >= l0, l0, zero)
        + jnp.where(tau >= e1, l1, zero)
        + jnp.where(tau >= e1 + l2, l2, zero)
    )


def cos_sin(base, freq_ref, len_ref, run):
    tau = base + lax.broadcasted_iota(jnp.int32, (BLOCK, HEAD_WIDTH), 0)
    pos = PROMPT_TOKENS + tau - begins_of(tau, len_ref, run)
    angle = pos.astype(f32) * freq_ref[0:1, :]
    lane = lax.broadcasted_iota(jnp.int32, (BLOCK, HEAD_WIDTH), 1)
    sine = jnp.sin(angle)
    return jnp.cos(angle), jnp.where(lane < 64, -sine, sine)


def send_in(
    q_ref, do_ref, k_ref, v_ref, len_ref, pk_ref, pv_ref, freq_ref,
    qx, dox, kvw, pt,
    qrot, kvs, ptile,
    q_s, q_r, d_s, d_r, kv_s, kv_r, f_s, f_r, g_s, g_r, p_s, p_r, loc,
):
    g, z, c = lax.axis_index("grp"), lax.axis_index("uly"), lax.axis_index("ctx")
    zr = lax.rem(z, RUN_PLACES)
    run = z // RUN_PLACES
    has_next, has_prev = zr < RUN_PLACES - 1, zr > 0
    relays = (zr == 1) | (zr == 2)
    gets_far = zr >= 2
    is_diag = z == c
    barrier = pltpu.get_barrier_semaphore()

    def greet(k, _):
        pl.semaphore_signal(barrier, inc=1, device_id=(g, z, lax.rem(c + k, N_CTX)), device_id_type=MESH)
        return 0

    lax.fori_loop(1, N_CTX, greet, 0)

    @pl.when(has_prev)
    def _():
        pl.semaphore_signal(barrier, inc=1, device_id=(g, z - 1, c), device_id_type=MESH)

    def greet_prompt(n, _):
        gg, cc = n // N_CTX, lax.rem(n, N_CTX)

        @pl.when(jnp.logical_not(is_diag & (gg == g) & (cc == c)))
        def _():
            pl.semaphore_signal(barrier, inc=1, device_id=(gg, c, cc), device_id_type=MESH)

        return 0

    lax.fori_loop(0, N_GRP * N_CTX, greet_prompt, 0)

    cosine, sine = cos_sin(zr * CHUNK + c * BLOCK, freq_ref, len_ref, run)

    def turned(block):
        x = block.astype(f32)
        return (x * cosine + pltpu.roll(x, 64, 1) * sine).astype(bf16)

    for j in range(KEY_VALUE_HEADS):
        kvs[:, 256 * j : 256 * j + 128] = turned(k_ref[:, 128 * j : 128 * j + 128])
        kvs[:, 256 * j + 128 : 256 * j + 256] = v_ref[:, 128 * j : 128 * j + 128]
    ptile[0:4, :] = pk_ref[...].astype(f32)
    ptile[4:8, :] = pv_ref[...].astype(f32)

    targets = (
        (N_CTX - 1)
        + jnp.where(has_next, 1, 0)
        + N_GRP * N_ULY
        - jnp.where(is_diag, 1, 0)
    )
    pl.semaphore_wait(barrier, targets)

    def remote(src, dst, s, r, dev):
        return pltpu.make_async_remote_copy(
            src_ref=src, dst_ref=dst, send_sem=s, recv_sem=r, device_id=dev, device_id_type=MESH
        )

    def rows(at):
        return pl.ds(pl.multiple_of(at, BLOCK), BLOCK)

    def kv_copy(peer):
        return remote(
            kvs.at[:, pl.ds(pl.multiple_of(peer * 256, 256), 256)],
            kvw.at[rows(2 * CHUNK + c * BLOCK), :],
            kv_s.at[peer], kv_r.at[c], (g, z, peer),
        )

    def kv_arrival(j):
        return remote(
            kvs.at[:, pl.ds(0, 256)], kvw.at[rows(2 * CHUNK + j * BLOCK), :],
            kv_s.at[j], kv_r.at[j], (g, z, j),
        )

    def d_copy(peer):
        return remote(
            do_ref.at[:, pl.ds(pl.multiple_of(peer * 512, 512), 512)],
            dox.at[rows(c * BLOCK), :], d_s.at[peer], d_r.at[c], (g, z, peer),
        )

    def d_arrival(j):
        return remote(
            do_ref.at[:, pl.ds(0, 512)], dox.at[rows(j * BLOCK), :], d_s.at[j], d_r.at[j], (g, z, j)
        )

    def q_copy(peer):
        return remote(
            qrot.at[:, pl.ds(pl.multiple_of(peer * 512, 512), 512)],
            qx.at[rows(c * BLOCK), :], q_s.at[peer], q_r.at[c], (g, z, peer),
        )

    def q_arrival(j):
        return remote(
            qrot.at[:, pl.ds(0, 512)], qx.at[rows(j * BLOCK), :], q_s.at[j], q_r.at[j], (g, z, j)
        )

    def own_copies():
        return (
            pltpu.make_async_copy(
                kvs.at[:, pl.ds(pl.multiple_of(c * 256, 256), 256)],
                kvw.at[rows(2 * CHUNK + c * BLOCK), :], loc.at[0],
            ),
            pltpu.make_async_copy(
                do_ref.at[:, pl.ds(pl.multiple_of(c * 512, 512), 512)],
                dox.at[rows(c * BLOCK), :], loc.at[1],
            ),
            pltpu.make_async_copy(
                qrot.at[:, pl.ds(pl.multiple_of(c * 512, 512), 512)],
                qx.at[rows(c * BLOCK), :], loc.at[2],
            ),
        )

    own_kv, own_d, own_q = own_copies()
    own_prompt = pltpu.make_async_copy(ptile, pt.at[g * N_CTX + c], loc.at[3])

    def start_kv(k, _):
        kv_copy(lax.rem(c + k, N_CTX)).start()
        return 0

    lax.fori_loop(1, N_CTX, start_kv, 0)
    own_kv.start()

    def prompt_copy(n):
        return remote(
            ptile, pt.at[g * N_CTX + c], p_s.at[n], p_r.at[g * N_CTX + c],
            (n // N_ULY, lax.rem(n, N_ULY), z),
        )

    def to_self(n):
        return is_diag & (n // N_ULY == g) & (lax.rem(n, N_ULY) == z)

    def from_self(n):
        return is_diag & (n // N_CTX == g) & (lax.rem(n, N_CTX) == c)

    def start_prompt(n, _):
        @pl.when(jnp.logical_not(to_self(n)))
        def _():
            prompt_copy(n).start()

        return 0

    lax.fori_loop(0, N_GRP * N_ULY, start_prompt, 0)

    @pl.when(is_diag)
    def _():
        own_prompt.start()

    def start_d(k, _):
        d_copy(lax.rem(c + k, N_CTX)).start()
        return 0

    lax.fori_loop(1, N_CTX, start_d, 0)
    own_d.start()

    def turn_heads(peer):
        for h in range(QH):
            at = pl.ds(pl.multiple_of(peer * 512 + h * 128, 128), 128)
            qrot[:, at] = turned(q_ref[:, at])

    def start_q(k, _):
        peer = lax.rem(c + k, N_CTX)
        turn_heads(peer)
        q_copy(peer).start()
        return 0

    lax.fori_loop(1, N_CTX, start_q, 0)
    turn_heads(c)
    own_q.start()

    def next_copy(j):
        return remote(
            kvw.at[rows(2 * CHUNK + j * BLOCK), :], kvw.at[rows(CHUNK + j * BLOCK), :],
            f_s.at[j], f_r.at[j], (g, jnp.where(has_next, z + 1, z - 1), c),
        )

    def far_copy(j):
        return remote(
            kvw.at[rows(CHUNK + j * BLOCK), :], kvw.at[rows(j * BLOCK), :],
            g_s.at[j], g_r.at[j], (g, jnp.where(has_next, z + 1, z - 1), c),
        )

    own_kv.wait()

    @pl.when(has_next)
    def _():
        next_copy(c).start()

    def pass_on(k, _):
        j = lax.rem(c + N_CTX - k, N_CTX)
        kv_arrival(j).wait_recv()

        @pl.when(has_next)
        def _():
            next_copy(j).start()

        return 0

    lax.fori_loop(1, N_CTX, pass_on, 0)

    def pass_far(k, _):
        j = lax.rem(c + N_CTX - k, N_CTX)

        @pl.when(has_prev)
        def _():
            next_copy(j).wait_recv()

        @pl.when(relays)
        def _():
            far_copy(j).start()

        return 0

    lax.fori_loop(0, N_CTX, pass_far, 0)

    def finish(k, _):
        j = lax.rem(c + k, N_CTX)
        kv_copy(j).wait_send()
        d_copy(j).wait_send()
        q_copy(j).wait_send()
        d_arrival(j).wait_recv()
        q_arrival(j).wait_recv()
        return 0

    lax.fori_loop(1, N_CTX, finish, 0)

    def finish_prompt(n, _):
        @pl.when(jnp.logical_not(to_self(n)))
        def _():
            prompt_copy(n).wait_send()

        @pl.when(jnp.logical_not(from_self(n)))
        def _():
            remote(ptile, pt.at[n], p_s.at[n], p_r.at[n], (n // N_ULY, lax.rem(n, N_ULY), z)).wait_recv()

        return 0

    lax.fori_loop(0, N_GRP * N_ULY, finish_prompt, 0)

    @pl.when(is_diag)
    def _():
        own_prompt.wait()

    own_d.wait()
    own_q.wait()

    def finish_far(j, _):
        @pl.when(has_next)
        def _():
            next_copy(j).wait_send()

        @pl.when(relays)
        def _():
            far_copy(j).wait_send()

        @pl.when(gets_far)
        def _():
            far_copy(j).wait_recv()

        return 0

    lax.fori_loop(0, N_CTX, finish_far, 0)


def dot_nt(a, b):
    return lax.dot_general(a, b, (((1,), (1,)), ((), ())), preferred_element_type=f32)


def dot_nn(a, b):
    return lax.dot_general(a, b, (((1,), (0,)), ((), ())), preferred_element_type=f32)


def dot_tn(a, b):
    return lax.dot_general(a, b, (((0,), (0,)), ((), ())), preferred_element_type=f32)


def attend(qx, dox, kvw, pt, len_ref, freq_t, ox, dqx, dkv, pg, s_all, kp, vp, pkg, pvg, o_t, dq_t):
    z = lax.axis_index("uly")
    zr = lax.rem(z, RUN_PLACES)
    run = z // RUN_PLACES
    start = zr * CHUNK
    for n in range(32):
        kp[4 * n : 4 * n + 4, :] = pt[n, 0:4, :]
        vp[4 * n : 4 * n + 4, :] = pt[n, 4:8, :]
    dkv[...] = jnp.zeros_like(dkv)
    pkg[...] = jnp.zeros_like(pkg)
    pvg[...] = jnp.zeros_like(pvg)

    def row_tile(r, _):
        t0 = r * TQ
        at_rows = pl.ds(pl.multiple_of(t0, TQ), TQ)
        q = jnp.concatenate([qx[at_rows, 128 * h : 128 * h + 128] for h in range(QH)], axis=0)
        do = jnp.concatenate([dox[at_rows, 128 * h : 128 * h + 128] for h in range(QH)], axis=0)
        tau = start + t0 + lax.broadcasted_iota(jnp.int32, (1, TQ), 1)
        begin = begins_of(tau, len_ref, run)
        pos = (PROMPT_TOKENS + tau - begin).astype(f32)
        to_win = 2 * CHUNK - start
        begin4 = jnp.concatenate([begin + to_win] * QH, axis=1)
        tau4 = jnp.concatenate([tau + to_win] * QH, axis=1)
        tile_hi = 2 * CHUNK // TK + r
        first = start + t0
        l0, l1, l2 = len_ref[run, 0], len_ref[run, 1], len_ref[run, 2]
        first_begin = (
            jnp.where(first >= l0, l0, 0)
            + jnp.where(first >= l0 + l1, l1, 0)
            + jnp.where(first >= l0 + l1 + l2, l2, 0)
        )
        tile_lo = (first_begin + to_win) // TK
        kpb, vpb = kp[...].astype(bf16), vp[...].astype(bf16)

        s = dot_nt(kpb, q)
        s_all[0:PROMPT_TOKENS, :] = s
        m0 = jnp.max(s, axis=0, keepdims=True)
        l_0 = jnp.sum(jnp.exp2((s - m0) * C2), axis=0, keepdims=True)

        def slot(kt):
            return pl.ds(pl.multiple_of(PROMPT_TOKENS + (kt - tile_lo) * TK, 128), TK)

        def keys(kt):
            return pl.ds(pl.multiple_of(kt * TK, TK), TK)

        def pass_a(kt, carry):
            m, l = carry
            s = dot_nt(kvw[keys(kt), 0:128], q)
            kidx = kt * TK + lax.broadcasted_iota(jnp.int32, (TK, LANES), 0)
            s = jnp.where((kidx >= begin4) & (kidx <= tau4), s, neg_fill)
            s_all[slot(kt), :] = s
            m_new = jnp.maximum(m, jnp.max(s, axis=0, keepdims=True))
            l = l * jnp.exp2((m - m_new) * C2) + jnp.sum(
                jnp.exp2((s - m_new) * C2), axis=0, keepdims=True
            )
            return m_new, l

        m, l = lax.fori_loop(tile_lo, tile_hi + 1, pass_a, (m0, l_0))
        inv_l = 1.0 / l

        def prob_of(s):
            return jnp.exp2((s - m) * C2) * inv_l

        p = prob_of(s_all[0:PROMPT_TOKENS, :])
        s_all[0:PROMPT_TOKENS, :] = p
        o_t[...] = dot_tn(vpb, p.astype(bf16))

        def pass_c(kt, _):
            p = prob_of(s_all[slot(kt), :])
            s_all[slot(kt), :] = p
            o_t[...] += dot_tn(kvw[keys(kt), 128:256], p.astype(bf16))
            return 0

        lax.fori_loop(tile_lo, tile_hi + 1, pass_c, 0)
        o = o_t[...].astype(bf16).astype(f32)
        delta = jnp.sum(o * do.astype(f32).T, axis=0, keepdims=True)
        o_rows = o.T.astype(bf16)
        for h in range(QH):
            ox[at_rows, 128 * h : 128 * h + 128] = o_rows[TQ * h : TQ * h + TQ, :]

        def grads(p, v):
            dp = dot_nt(v, do)
            return (p * (dp - delta) * SCALE).astype(bf16)

        p = s_all[0:PROMPT_TOKENS, :]
        ds = grads(p, vpb)
        dq_t[...] = dot_tn(kpb, ds)
        pkg[...] += dot_nn(ds, q)
        pvg[...] += dot_nn(p.astype(bf16), do)

        def pass_d(kt, _):
            p = s_all[slot(kt), :]
            ds = grads(p, kvw[keys(kt), 128:256])
            dq_t[...] += dot_tn(kvw[keys(kt), 0:128], ds)
            dkv[keys(kt), 0:128] += dot_nn(ds, q)
            dkv[keys(kt), 128:256] += dot_nn(p.astype(bf16), do)
            return 0

        lax.fori_loop(tile_lo, tile_hi + 1, pass_d, 0)
        angle = freq_t[...] * pos
        cosine = jnp.concatenate([jnp.cos(angle)] * QH, axis=1)
        sine = jnp.concatenate([jnp.sin(angle)] * QH, axis=1)
        x1, x2 = dq_t[0:64, :], dq_t[64:128, :]
        back = jnp.concatenate([x1 * cosine + x2 * sine, x2 * cosine - x1 * sine], axis=0)
        back = back.T.astype(bf16)
        for h in range(QH):
            dqx[at_rows, 128 * h : 128 * h + 128] = back[TQ * h : TQ * h + TQ, :]
        return 0

    lax.fori_loop(0, CHUNK // TQ, row_tile, 0)
    for n in range(32):
        pg[n, 0:4, :] = pkg[4 * n : 4 * n + 4, :]
        pg[n, 4:8, :] = pvg[4 * n : 4 * n + 4, :]


def send_out(
    ox, dqx, dkv, pg, len_ref, freq_ref,
    out, dq, dk, dv, dpk, dpv,
    far_out, far_in, near_out, near_in, own, pin, cosines, sines,
    o_s, o_r, q_s, q_r, f_s, f_r, n_s, n_r, k_s, k_r, v_s, v_r, p_s, p_r, loc,
):
    g, z, c = lax.axis_index("grp"), lax.axis_index("uly"), lax.axis_index("ctx")
    zr = lax.rem(z, RUN_PLACES)
    run = z // RUN_PLACES
    has_next, has_prev = zr < RUN_PLACES - 1, zr > 0
    gets_far = (zr == 1) | (zr == 2)
    sends_far = zr >= 2
    is_diag = z == c
    barrier = pltpu.get_barrier_semaphore()

    def greet(k, _):
        pl.semaphore_signal(barrier, inc=1, device_id=(g, z, lax.rem(c + k, N_CTX)), device_id_type=MESH)
        return 0

    lax.fori_loop(1, N_CTX, greet, 0)

    @pl.when(has_next)
    def _():
        pl.semaphore_signal(barrier, inc=1, device_id=(g, z + 1, c), device_id_type=MESH)

    def greet_prompt(n, _):
        gg, zz = n // N_ULY, lax.rem(n, N_ULY)

        @pl.when(jnp.logical_not(is_diag & (gg == g) & (zz == z)))
        def _():
            pl.semaphore_signal(barrier, inc=1, device_id=(gg, zz, z), device_id_type=MESH)

        return 0

    lax.fori_loop(0, N_GRP * N_ULY, greet_prompt, 0)

    def rows(at):
        return pl.ds(pl.multiple_of(at, BLOCK), BLOCK)

    far_out[...] = dkv[0:CHUNK, :].astype(bf16)

    targets = (
        (N_CTX - 1)
        + jnp.where(has_prev, 1, 0)
        + N_GRP * N_ULY
        - jnp.where(is_diag, 1, 0)
    )
    pl.semaphore_wait(barrier, targets)

    def remote(src, dst, s, r, dev):
        return pltpu.make_async_remote_copy(
            src_ref=src, dst_ref=dst, send_sem=s, recv_sem=r, device_id=dev, device_id_type=MESH
        )

    below = jnp.where(has_prev, z - 1, z + 1)

    def far_copy(j):
        return remote(
            far_out.at[rows(j * BLOCK), :], far_in.at[rows(j * BLOCK), :],
            f_s.at[j], f_r.at[j], (g, below, c),
        )

    def near_copy(j):
        return remote(
            near_out.at[rows(j * BLOCK), :], near_in.at[rows(j * BLOCK), :],
            n_s.at[j], n_r.at[j], (g, below, c),
        )

    def start_far(j, _):
        @pl.when(sends_far)
        def _():
            far_copy(j).start()

        return 0

    lax.fori_loop(0, N_CTX, start_far, 0)

    def block_copy(src, dst, s, r, width, peer):
        return remote(
            src.at[rows(peer * BLOCK), :],
            dst.at[:, pl.ds(pl.multiple_of(c * width, width), width)],
            s.at[peer], r.at[c], (g, z, peer),
        )

    def block_arrival(src, dst, s, r, width, j):
        return remote(
            src.at[rows(j * BLOCK), :],
            dst.at[:, pl.ds(pl.multiple_of(j * width, width), width)],
            s.at[j], r.at[j], (g, z, j),
        )

    def start_o(k, _):
        block_copy(ox, out, o_s, o_r, 512, lax.rem(c + k, N_CTX)).start()
        return 0

    def start_dq(k, _):
        block_copy(dqx, dq, q_s, q_r, 512, lax.rem(c + k, N_CTX)).start()
        return 0

    def own_copy(src, dst, width, at):
        return pltpu.make_async_copy(
            src.at[rows(c * BLOCK), :],
            dst.at[:, pl.ds(pl.multiple_of(c * width, width), width)], loc.at[at],
        )

    def to_self(n):
        return is_diag & (n // N_CTX == g) & (lax.rem(n, N_CTX) == c)

    def from_self(n):
        return is_diag & (n // N_ULY == g) & (lax.rem(n, N_ULY) == z)

    me = g * N_ULY + z

    def prompt_copy(n):
        return remote(
            pg.at[n], pin.at[me], p_s.at[n], p_r.at[me], (n // N_CTX, c, lax.rem(n, N_CTX))
        )

    def start_prompt(n, _):
        @pl.when(jnp.logical_not(to_self(n)))
        def _():
            prompt_copy(n).start()

        return 0

    lax.fori_loop(0, N_GRP * N_CTX, start_prompt, 0)
    own_prompt = pltpu.make_async_copy(pg.at[g * N_CTX + c], pin.at[me], loc.at[0])

    @pl.when(is_diag)
    def _():
        own_prompt.start()

    lax.fori_loop(1, N_CTX, start_o, 0)
    lax.fori_loop(1, N_CTX, start_dq, 0)
    own_copy(ox, out, 512, 1).start()
    own_copy(dqx, dq, 512, 2).start()

    def table(j, _):
        cosine, sine = cos_sin(zr * CHUNK + j * BLOCK, freq_ref, len_ref, run)
        cosines[rows(j * BLOCK), :] = cosine
        sines[rows(j * BLOCK), :] = sine
        return 0

    lax.fori_loop(0, N_CTX, table, 0)

    def near(j, _):
        mine = dkv[rows(CHUNK + j * BLOCK), :]

        @pl.when(gets_far)
        def _():
            far_copy(j).wait_recv()
            near_out[rows(j * BLOCK), :] = (mine + far_in[rows(j * BLOCK), :].astype(f32)).astype(bf16)

        @pl.when(jnp.logical_not(gets_far))
        def _():
            near_out[rows(j * BLOCK), :] = mine.astype(bf16)

        @pl.when(has_prev)
        def _():
            near_copy(j).start()

        return 0

    lax.fori_loop(0, N_CTX, near, 0)

    def finish_block(total, j):
        x = total[:, 0:128]
        cosine, sine = cosines[rows(j * BLOCK), :], sines[rows(j * BLOCK), :]
        own[0, rows(j * BLOCK), :] = (x * cosine - pltpu.roll(x, 64, 1) * sine).astype(bf16)
        own[1, rows(j * BLOCK), :] = total[:, 128:256].astype(bf16)

    def home(k, _):
        j = lax.rem(c + k, N_CTX)
        mine = dkv[rows(2 * CHUNK + j * BLOCK), :]

        @pl.when(has_next)
        def _():
            near_copy(j).wait_recv()
            finish_block(mine + near_in[rows(j * BLOCK), :].astype(f32), j)

        @pl.when(jnp.logical_not(has_next))
        def _():
            finish_block(mine, j)

        @pl.when(k < N_CTX)
        def _():
            block_copy(own.at[0], dk, k_s, k_r, 128, j).start()
            block_copy(own.at[1], dv, v_s, v_r, 128, j).start()

        return 0

    lax.fori_loop(1, N_CTX + 1, home, 0)
    own_copy(own.at[0], dk, 128, 3).start()
    own_copy(own.at[1], dv, 128, 4).start()

    def finish_prompt(n, _):
        @pl.when(jnp.logical_not(to_self(n)))
        def _():
            prompt_copy(n).wait_send()

        @pl.when(jnp.logical_not(from_self(n)))
        def _():
            remote(pg.at[n], pin.at[n], p_s.at[n], p_r.at[n], (n // N_CTX, c, lax.rem(n, N_CTX))).wait_recv()

        return 0

    lax.fori_loop(0, N_GRP * N_CTX, finish_prompt, 0)

    @pl.when(is_diag)
    def _():
        own_prompt.wait()

    total = jnp.sum(pin[...], axis=0)
    dpk[...] = total[0:4, :].astype(bf16)
    dpv[...] = total[4:8, :].astype(bf16)

    def finish(k, _):
        j = lax.rem(c + k, N_CTX)
        for src, dst, s, r, width in (
            (ox, out, o_s, o_r, 512),
            (dqx, dq, q_s, q_r, 512),
            (own.at[0], dk, k_s, k_r, 128),
            (own.at[1], dv, v_s, v_r, 128),
        ):
            block_copy(src, dst, s, r, width, j).wait_send()
            block_arrival(src, dst, s, r, width, j).wait_recv()
        return 0

    lax.fori_loop(1, N_CTX, finish, 0)
    own_copy(ox, out, 512, 1).wait()
    own_copy(dqx, dq, 512, 2).wait()
    own_copy(own.at[0], dk, 128, 3).wait()
    own_copy(own.at[1], dv, 128, 4).wait()

    def finish_z(j, _):
        @pl.when(sends_far)
        def _():
            far_copy(j).wait_send()

        @pl.when(has_prev)
        def _():
            near_copy(j).wait_send()

        return 0

    lax.fori_loop(0, N_CTX, finish_z, 0)


def spec(space):
    return pl.BlockSpec(memory_space=space)


VMEM, SMEM, ANY = pltpu.VMEM, pltpu.SMEM, pl.ANY
DMA = pltpu.SemaphoreType.DMA


def local(queries, keys_in, values_in, out_grad, lengths, prompt_keys, prompt_values):
    sds = jax.ShapeDtypeStruct
    lens = lengths[0]
    freq = frequencies()
    freq_row = jnp.asarray(np.tile(freq[None, :], (8, 1)))
    freq_col = jnp.asarray(np.tile(freq[:64, None], (1, TQ)))
    qx, dox, kvw, pt = pl.pallas_call(
        send_in,
        out_shape=(
            sds((CHUNK, 512), bf16),
            sds((CHUNK, 512), bf16),
            sds((WIN, 256), bf16),
            sds((32, 8, 128), f32),
        ),
        in_specs=[spec(VMEM), spec(ANY), spec(VMEM), spec(VMEM), spec(SMEM), spec(VMEM), spec(VMEM), spec(VMEM)],
        out_specs=(spec(ANY),) * 4,
        scratch_shapes=[
            VMEM((BLOCK, 4096), bf16),
            VMEM((BLOCK, 2048), bf16),
            VMEM((8, 128), f32),
        ]
        + [DMA((8,))] * 10
        + [DMA((32,))] * 2
        + [DMA((4,))],
        compiler_params=pltpu.CompilerParams(
            collective_id=0, has_side_effects=True, vmem_limit_bytes=32 << 20
        ),
        name="send_in",
    )(queries, out_grad, keys_in, values_in, lens, prompt_keys, prompt_values, freq_row)

    ox, dqx, dkv, pg = pl.pallas_call(
        attend,
        out_shape=(
            sds((CHUNK, 512), bf16),
            sds((CHUNK, 512), bf16),
            sds((WIN, 256), f32),
            sds((32, 8, 128), f32),
        ),
        in_specs=[spec(VMEM), spec(VMEM), spec(VMEM), spec(VMEM), spec(SMEM), spec(VMEM)],
        out_specs=(spec(VMEM),) * 4,
        scratch_shapes=[
            VMEM((PROMPT_TOKENS + 9 * TK, LANES), f32),
            VMEM((128, 128), f32),
            VMEM((128, 128), f32),
            VMEM((128, 128), f32),
            VMEM((128, 128), f32),
            VMEM((128, LANES), f32),
            VMEM((128, LANES), f32),
        ],
        compiler_params=pltpu.CompilerParams(vmem_limit_bytes=48 << 20),
        name="attend",
    )(qx, dox, kvw, pt, lens, freq_col)

    return pl.pallas_call(
        send_out,
        out_shape=(
            sds((BLOCK, 4096), bf16),
            sds((BLOCK, 4096), bf16),
            sds((BLOCK, 1024), bf16),
            sds((BLOCK, 1024), bf16),
            sds((4, 128), bf16),
            sds((4, 128), bf16),
        ),
        in_specs=[spec(ANY), spec(ANY), spec(VMEM), spec(ANY), spec(SMEM), spec(VMEM)],
        out_specs=(spec(ANY),) * 4 + (spec(VMEM),) * 2,
        scratch_shapes=[
            VMEM((CHUNK, 256), bf16),
            VMEM((CHUNK, 256), bf16),
            VMEM((CHUNK, 256), bf16),
            VMEM((CHUNK, 256), bf16),
            VMEM((2, CHUNK, 128), bf16),
            VMEM((32, 8, 128), f32),
            VMEM((CHUNK, 128), f32),
            VMEM((CHUNK, 128), f32),
        ]
        + [DMA((8,))] * 12
        + [DMA((32,))] * 2
        + [DMA((8,))],
        compiler_params=pltpu.CompilerParams(
            collective_id=1, has_side_effects=True, vmem_limit_bytes=32 << 20
        ),
        name="send_out",
    )(ox, dqx, dkv, pg, lens, freq_row)


def solution(mesh):
    tokens = P(("grp", "uly", "ctx"), None)
    prompt = P(("grp", "ctx"), "uly")
    in_specs = (tokens, tokens, tokens, tokens, P("grp", None, None), prompt, prompt)
    out_specs = (tokens, tokens, tokens, tokens, prompt, prompt)
    return jax.shard_map(local, mesh=mesh, in_specs=in_specs, out_specs=out_specs, check_vma=False)
```

```python
import jax
import jax.numpy as jnp
from jax import lax
from jax.experimental import pallas as pl
from jax.experimental.pallas import tpu as pltpu
from jax.sharding import PartitionSpec as P

H = 32
KEY_VALUE_HEADS = 8
HEAD_WIDTH = 128
PROMPT_TOKENS = 128
theta_base = 1000000.0
neg_fill = -1e30

N_GRP, N_ULY, N_CTX = 4, 8, 8
N_ALL = N_GRP * N_CTX
BLOCK = 128
CHUNK = N_CTX * BLOCK
RUN_PLACES = 4
QH = H // KEY_VALUE_HEADS
WIN = 3 * CHUNK
OWN = 2 * CHUNK
TQ = 256
ROW_TILES = CHUNK // TQ
LANES = QH * TQ
STEP = 512
HEAD_KEYS = PROMPT_TOKENS + TQ
HEAD_AT = WIN - TQ
SCALE = HEAD_WIDTH**-0.5
LOG2E = 1.4426950408889634
C2 = SCALE * LOG2E
MESH = pl.DeviceIdType.MESH
f32, bf16, i32 = jnp.float32, jnp.bfloat16, jnp.int32


def frequency_of(index):
    out = jnp.ones(index.shape, f32)
    for bit in range(6):
        power = theta_base ** (-(2.0 * 2**bit) / HEAD_WIDTH)
        out = out * jnp.where((index // 2**bit) % 2 == 1, f32(power), f32(1.0))
    return out


def begins_of(tau, lens):
    l0, l1, l2 = lens
    zero = jnp.zeros_like(tau)
    return (
        jnp.where(tau >= l0, l0, zero)
        + jnp.where(tau >= l0 + l1, l1, zero)
        + jnp.where(tau >= l0 + l1 + l2, l2, zero)
    )


def cos_sin(base, lens):
    tau = base + lax.broadcasted_iota(i32, (BLOCK, HEAD_WIDTH), 0)
    pos = PROMPT_TOKENS + tau - begins_of(tau, lens)
    lane = lax.broadcasted_iota(i32, (BLOCK, HEAD_WIDTH), 1)
    freq = frequency_of(lax.broadcasted_iota(i32, (8, HEAD_WIDTH), 1) % 64)[0:1, :]
    angle = pos.astype(f32) * freq
    sine = jnp.sin(angle)
    return jnp.cos(angle), jnp.where(lane < 64, -sine, sine)


def membership(base, lens, count):
    l0, l1, l2 = lens
    tau = base + lax.broadcasted_iota(i32, (count, HEAD_WIDTH), 0)
    lane = lax.broadcasted_iota(i32, (count, HEAD_WIDTH), 1)
    low = jnp.where(lane == 0, 0, jnp.where(lane == 1, l0, l0 + l1))
    high = jnp.where(lane == 0, l0, jnp.where(lane == 1, l0 + l1, l0 + l1 + l2))
    return (tau >= low) & (tau < high), lane


def dot_nt(a, b):
    return lax.dot_general(a, b, (((1,), (1,)), ((), ())), preferred_element_type=f32)


def dot_nn(a, b):
    return lax.dot_general(a, b, (((1,), (0,)), ((), ())), preferred_element_type=f32)


def dot_tn(a, b):
    return lax.dot_general(a, b, (((0,), (0,)), ((), ())), preferred_element_type=f32)


def step_kernel(
    q_hbm, do_hbm, k_hbm, v_hbm, len_ref, pk_ref, pv_ref,
    out, dq, dk, dv, dpk, dpv,
    q_in, k_in, v_in, qrot, kvs, ptile, pt, qx, dox, kvw, aug, onehot, qst, dost, kp, vp,
    s_all, o_t, dq_all, stats, dkv, pkg, pvg, pg, pin, ox, dqx,
    far_out, far_in, near_out, near_in, own, cosines, sines,
    q_s, q_r, d_s, d_r, kv_s, kv_r, f_s, f_r, g_s, g_r, o_s, o_r, dq_s, dq_r,
    fo_s, fo_r, no_s, no_r, k_s, k_r, v_s, v_r, p_s, p_r, pg_s, pg_r, loc,
):
    g, z, c = lax.axis_index("grp"), lax.axis_index("uly"), lax.axis_index("ctx")
    zr = lax.rem(z, RUN_PLACES)
    run = z // RUN_PLACES
    start = zr * CHUNK
    has_next, has_prev = zr < RUN_PLACES - 1, zr > 0
    middle = (zr == 1) | (zr == 2)
    has_far = zr >= 2
    is_diag = z == c
    lens = (len_ref[run, 0], len_ref[run, 1], len_ref[run, 2])
    barrier = pltpu.get_barrier_semaphore()

    def loop(low, high, body):
        def run_body(i, _):
            body(i)
            return 0

        lax.fori_loop(low, high, run_body, 0)

    def rows(at):
        return pl.ds(pl.multiple_of(at, BLOCK), BLOCK)

    def columns(at, width):
        return pl.ds(pl.multiple_of(at * width, width), width)

    def remote(src, dst, s, r, dev):
        return pltpu.make_async_remote_copy(
            src_ref=src, dst_ref=dst, send_sem=s, recv_sem=r, device_id=dev, device_id_type=MESH
        )

    load_k = pltpu.make_async_copy(k_hbm, k_in, loc.at[0])
    load_v = pltpu.make_async_copy(v_hbm, v_in, loc.at[1])
    load_q = pltpu.make_async_copy(q_hbm, q_in, loc.at[2])
    load_k.start()
    load_v.start()
    load_q.start()

    def greet(dev):
        pl.semaphore_signal(barrier, inc=1, device_id=dev, device_id_type=MESH)

    loop(1, N_CTX, lambda k: greet((g, z, lax.rem(c + k, N_CTX))))

    @pl.when(has_prev)
    def _():
        greet((g, z - 1, c))

    @pl.when(has_next)
    def _():
        greet((g, z + 1, c))

    def at_row(n):
        return n // N_CTX, c, lax.rem(n, N_CTX)

    def at_column(n):
        return n // N_ULY, lax.rem(n, N_ULY), z

    def row_is_me(n):
        return is_diag & (n // N_CTX == g) & (lax.rem(n, N_CTX) == c)

    def column_is_me(n):
        return is_diag & (n // N_ULY == g) & (lax.rem(n, N_ULY) == z)

    def greet_families(n):
        @pl.when(jnp.logical_not(row_is_me(n)))
        def _():
            greet(at_row(n))

        @pl.when(jnp.logical_not(column_is_me(n)))
        def _():
            greet(at_column(n))

    loop(0, N_ALL, greet_families)

    cosine, sine = cos_sin(start + c * BLOCK, lens)

    def turned(block):
        x = block.astype(f32)
        return (x * cosine + pltpu.roll(x, 64, 1) * sine).astype(bf16)

    load_k.wait()
    load_v.wait()
    for j in range(KEY_VALUE_HEADS):
        kvs[:, 256 * j : 256 * j + 128] = turned(k_in[:, 128 * j : 128 * j + 128])
        kvs[:, 256 * j + 128 : 256 * j + 256] = v_in[:, 128 * j : 128 * j + 128]
    ptile[0:4, :] = pk_ref[...].astype(f32)
    ptile[4:8, :] = pv_ref[...].astype(f32)

    pl.semaphore_wait(
        barrier,
        (N_CTX - 1)
        + jnp.where(has_next, 1, 0)
        + jnp.where(has_prev, 1, 0)
        + 2 * (N_ALL - jnp.where(is_diag, 1, 0)),
    )

    def spread(src, width, dst, base, s, r, peer):
        return remote(
            src.at[:, columns(peer, width)], dst.at[rows(base + c * BLOCK), :],
            s.at[peer], r.at[c], (g, z, peer),
        )

    def spread_in(src, width, dst, base, s, r, j):
        return remote(
            src.at[:, columns(j, width)], dst.at[rows(base + j * BLOCK), :], s.at[j], r.at[j], (g, z, j)
        )

    def spread_own(src, width, dst, base, at):
        return pltpu.make_async_copy(
            src.at[:, columns(c, width)], dst.at[rows(base + c * BLOCK), :], loc.at[at]
        )

    kv_way = (kvs, 256, kvw, OWN)
    d_way = (do_hbm, 512, dox, 0)
    q_way = (qrot, 512, qx, 0)
    loop(1, N_CTX, lambda k: spread(*kv_way, kv_s, kv_r, lax.rem(c + k, N_CTX)).start())
    spread_own(*kv_way, 3).start()
    me_in, me_back = g * N_CTX + c, g * N_ULY + z

    def prompt_copy(n):
        return remote(ptile, pt.at[me_in], p_s.at[n], p_r.at[me_in], at_column(n))

    def start_prompt(n):
        @pl.when(jnp.logical_not(column_is_me(n)))
        def _():
            prompt_copy(n).start()

    loop(0, N_ALL, start_prompt)
    own_prompt = pltpu.make_async_copy(ptile, pt.at[me_in], loc.at[4])

    @pl.when(is_diag)
    def _():
        own_prompt.start()

    loop(1, N_CTX, lambda k: spread(*d_way, d_s, d_r, lax.rem(c + k, N_CTX)).start())
    spread_own(*d_way, 5).start()
    load_q.wait()

    def turn_heads(peer):
        for h in range(QH):
            at = columns(peer * QH + h, 128)
            qrot[:, at] = turned(q_in[:, at])

    def start_q(k):
        peer = lax.rem(c + k, N_CTX)
        turn_heads(peer)
        spread(*q_way, q_s, q_r, peer).start()

    loop(1, N_CTX, start_q)
    turn_heads(c)
    spread_own(*q_way, 6).start()

    above = jnp.where(has_next, z + 1, z - 1)
    below = jnp.where(has_prev, z - 1, z + 1)

    def next_copy(j):
        return remote(
            kvw.at[rows(OWN + j * BLOCK), :], kvw.at[rows(CHUNK + j * BLOCK), :],
            f_s.at[j], f_r.at[j], (g, above, c),
        )

    def relay_copy(j):
        return remote(
            kvw.at[rows(CHUNK + j * BLOCK), :], kvw.at[rows(j * BLOCK), :],
            g_s.at[j], g_r.at[j], (g, above, c),
        )

    spread_own(*kv_way, 3).wait()

    @pl.when(has_next)
    def _():
        next_copy(c).start()

    def pass_on(k):
        j = lax.rem(c + N_CTX - k, N_CTX)
        spread_in(*kv_way, kv_s, kv_r, j).wait_recv()

        @pl.when(has_next)
        def _():
            next_copy(j).start()

    loop(1, N_CTX, pass_on)

    def tables(j):
        cosine_j, sine_j = cos_sin(start + j * BLOCK, lens)
        cosines[rows(j * BLOCK), :] = cosine_j
        sines[rows(j * BLOCK), :] = sine_j

    loop(0, N_CTX, tables)

    def key_masks(j):
        inside, lane = membership(start + j * BLOCK - OWN, lens, BLOCK)
        aug[rows(j * BLOCK), :] = jnp.where(inside | (lane >= 3), 0.0, neg_fill).astype(bf16)

    loop(0, WIN // BLOCK, key_masks)

    def query_masks(r):
        inside, lane = membership(start + r * TQ, lens, TQ)
        hot = jnp.where(inside & (lane < 3), 1.0, 0.0).astype(bf16)
        for h in range(QH):
            onehot[pl.ds(pl.multiple_of(r * LANES + h * TQ, TQ), TQ), :] = hot

    loop(0, ROW_TILES, query_masks)
    def clear(j):
        dkv[rows(j * BLOCK), :] = jnp.zeros((BLOCK, 256), f32)

    loop(0, WIN // BLOCK, clear)

    def take_prompt(n):
        @pl.when(jnp.logical_not(row_is_me(n)))
        def _():
            remote(ptile, pt.at[n], p_s.at[n], p_r.at[n], at_row(n)).wait_recv()

    loop(0, N_ALL, take_prompt)

    @pl.when(is_diag)
    def _():
        own_prompt.wait()

    for n in range(N_ALL):
        kp[4 * n : 4 * n + 4, :] = pt[n, 0:4, :]
        vp[4 * n : 4 * n + 4, :] = pt[n, 4:8, :]

    def pass_far(k):
        j = lax.rem(k + 4, N_CTX)

        @pl.when(has_prev)
        def _():
            next_copy(j).wait_recv()

        @pl.when(middle)
        def _():
            relay_copy(j).start()

    loop(0, N_CTX, pass_far)
    spread_own(*d_way, 5).wait()
    spread_own(*q_way, 6).wait()

    def keys_at(at, count):
        return pl.ds(pl.multiple_of(at, 256), count)

    def tile_rows(r):
        return pl.ds(pl.multiple_of(r * LANES, LANES), LANES)

    def masked_queries(r):
        return jnp.concatenate([onehot[tile_rows(r), :], qst[tile_rows(r), :]], axis=1)

    def masked_keys(at, count):
        return jnp.concatenate([aug[keys_at(at, count), :], kvw[keys_at(at, count), 0:128]], axis=1)

    def head_keys(r):
        first = jnp.concatenate([jnp.zeros((PROMPT_TOKENS, 128), bf16), kp[...].astype(bf16)], axis=1)
        return jnp.concatenate([first, masked_keys(OWN + r * TQ, TQ)], axis=0)

    def head_values(r):
        return jnp.concatenate([vp[...].astype(bf16), kvw[keys_at(OWN + r * TQ, TQ), 128:256]], axis=0)

    def head_scores(r, qa):
        s = dot_nt(head_keys(r), qa)
        key = lax.broadcasted_iota(i32, (HEAD_KEYS, LANES), 0) - PROMPT_TOKENS
        token = lax.broadcasted_iota(i32, (HEAD_KEYS, LANES), 1) % TQ
        return jnp.where(key <= token, s, neg_fill)

    head_at = pl.ds(HEAD_AT, HEAD_KEYS)

    def first_step(r):
        return jnp.where(has_far, r // 2, jnp.where(has_prev, CHUNK // STEP, OWN // STEP))

    def forward(k):
        r = ROW_TILES - 1 - k

        @pl.when(has_far & (lax.rem(k, 2) == 0))
        def _():
            loop(0, 4, lambda j: relay_copy(4 - 2 * k + j).wait_recv())

        for e in range(2):
            j = 2 * r + e

            @pl.when(j != c)
            def _():
                spread_in(*d_way, d_s, d_r, j).wait_recv()
                spread_in(*q_way, q_s, q_r, j).wait_recv()

        at_rows = pl.ds(pl.multiple_of(r * TQ, TQ), TQ)
        for h in range(QH):
            to = pl.ds(pl.multiple_of(r * LANES + h * TQ, TQ), TQ)
            qst[to, :] = qx[at_rows, 128 * h : 128 * h + 128]
            dost[to, :] = dox[at_rows, 128 * h : 128 * h + 128]
        qa = masked_queries(r)
        low = first_step(r)

        s = head_scores(r, qa)
        s_all[head_at, :] = s
        top = jnp.max(s, axis=0, keepdims=True)

        def score(at, count, top):
            s = dot_nt(masked_keys(at, count), qa)
            s_all[keys_at(at, count), :] = s
            return jnp.maximum(top, jnp.max(s, axis=0, keepdims=True))

        top = lax.fori_loop(0, r, lambda t, a: score(OWN + t * TQ, TQ, a), top)
        top = lax.fori_loop(low, OWN // STEP, lambda t, a: score(t * STEP, STEP, a), top)
        top = top * C2

        def power(at, total):
            p = jnp.exp2(s_all[at, :] * C2 - top)
            s_all[at, :] = p
            return total + jnp.sum(p, axis=0, keepdims=True)

        total = power(head_at, jnp.zeros((1, LANES), f32))
        total = lax.fori_loop(0, r, lambda t, a: power(keys_at(OWN + t * TQ, TQ), a), total)
        total = lax.fori_loop(low, OWN // STEP, lambda t, a: power(keys_at(t * STEP, STEP), a), total)
        inverse = 1.0 / total
        o_t[...] = dot_tn(head_values(r), (s_all[head_at, :] * inverse).astype(bf16))

        def gather(at, count):
            half = (s_all[keys_at(at, count), :] * inverse).astype(bf16)
            o_t[...] += dot_tn(kvw[keys_at(at, count), 128:256], half)

        loop(0, r, lambda t: gather(OWN + t * TQ, TQ))
        loop(low, OWN // STEP, lambda t: gather(t * STEP, STEP))
        o = o_t[...].astype(bf16).astype(f32)
        delta = jnp.sum(o * dost[tile_rows(r), :].astype(f32).T, axis=0, keepdims=True)
        stats[r, 0:1, :] = top + jnp.log(total) * LOG2E
        stats[r, 1:2, :] = delta
        o_rows = o.T.astype(bf16)
        for h in range(QH):
            ox[at_rows, 128 * h : 128 * h + 128] = o_rows[TQ * h : TQ * h + TQ, :]
        dq_all[r] = jnp.zeros((128, LANES), f32)
        send_rows(ox, out, o_s, o_r, r, 7)

    def home(src, dst, s, r, width, peer):
        return remote(
            src.at[rows(peer * BLOCK), :], dst.at[:, columns(c, width)], s.at[peer], r.at[c], (g, z, peer)
        )

    def home_in(src, dst, s, r, width, j):
        return remote(
            src.at[rows(j * BLOCK), :], dst.at[:, columns(j, width)], s.at[j], r.at[j], (g, z, j)
        )

    def home_own(src, dst, width, at):
        return pltpu.make_async_copy(src.at[rows(c * BLOCK), :], dst.at[:, columns(c, width)], loc.at[at])

    def send_rows(src, dst, s, rs, r, at):
        for e in range(2):
            j = 2 * r + e

            @pl.when(j != c)
            def _():
                home(src, dst, s, rs, 512, j).start()

            @pl.when(j == c)
            def _():
                home_own(src, dst, 512, at).start()

    loop(0, ROW_TILES, forward)

    def grads(r, s, v):
        p = jnp.exp2(s * C2 - stats[r, 0:1, :])
        dp = dot_nt(v, dost[tile_rows(r), :])
        ds = (p * (dp - stats[r, 1:2, :]) * SCALE).astype(bf16)
        return p.astype(bf16), ds

    def backward(r, at, count):
        s = dot_nt(masked_keys(at, count), masked_queries(r))
        here = keys_at(at, count)
        half, ds = grads(r, s, kvw[here, 128:256])
        dq_all[r] += dot_tn(kvw[here, 0:128], ds)
        dkv[here, 0:128] += dot_nn(ds, qst[tile_rows(r), :])
        dkv[here, 128:256] += dot_nn(half, dost[tile_rows(r), :])

    @pl.when(has_far)
    def _():
        def far_rows(r):
            loop(r // 2, CHUNK // STEP, lambda t: backward(r, t * STEP, STEP))

        loop(0, ROW_TILES, far_rows)

    def far_copy(j):
        return remote(
            far_out.at[rows(j * BLOCK), :], far_in.at[rows(j * BLOCK), :], fo_s.at[j], fo_r.at[j], (g, below, c)
        )

    def near_copy(j):
        return remote(
            near_out.at[rows(j * BLOCK), :], near_in.at[rows(j * BLOCK), :], no_s.at[j], no_r.at[j], (g, below, c)
        )

    def send_far(j):
        @pl.when(has_far)
        def _():
            far_out[rows(j * BLOCK), :] = dkv[rows(j * BLOCK), :].astype(bf16)
            far_copy(j).start()

    loop(0, N_CTX, send_far)

    @pl.when(has_prev)
    def _():
        def near_rows(r):
            loop(CHUNK // STEP, OWN // STEP, lambda t: backward(r, t * STEP, STEP))

        loop(0, ROW_TILES, near_rows)

    def send_near(j):
        mine = dkv[rows(CHUNK + j * BLOCK), :]

        @pl.when(middle)
        def _():
            far_copy(j).wait_recv()
            near_out[rows(j * BLOCK), :] = (mine + far_in[rows(j * BLOCK), :].astype(f32)).astype(bf16)

        @pl.when(jnp.logical_not(middle))
        def _():
            near_out[rows(j * BLOCK), :] = mine.astype(bf16)

        @pl.when(has_prev)
        def _():
            near_copy(j).start()

    loop(0, N_CTX, send_near)

    pkg[...] = jnp.zeros((128, 128), f32)
    pvg[...] = jnp.zeros((128, 128), f32)

    def own_rows(k):
        r = lax.rem(c // 2 + k, ROW_TILES)
        loop(0, r, lambda t: backward(r, OWN + t * TQ, TQ))
        s = head_scores(r, masked_queries(r))
        half, ds = grads(r, s, head_values(r))
        k_head = jnp.concatenate([kp[...].astype(bf16), kvw[keys_at(OWN + r * TQ, TQ), 0:128]], axis=0)
        back = dq_all[r] + dot_tn(k_head, ds)
        k_part = dot_nn(ds, qst[tile_rows(r), :])
        v_part = dot_nn(half, dost[tile_rows(r), :])
        pkg[...] += k_part[0:PROMPT_TOKENS, :]
        pvg[...] += v_part[0:PROMPT_TOKENS, :]
        here = keys_at(OWN + r * TQ, TQ)
        dkv[here, 0:128] += k_part[PROMPT_TOKENS:HEAD_KEYS, :]
        dkv[here, 128:256] += v_part[PROMPT_TOKENS:HEAD_KEYS, :]
        tau = start + r * TQ + lax.broadcasted_iota(i32, (1, TQ), 1)
        pos = (PROMPT_TOKENS + tau - begins_of(tau, lens)).astype(f32)
        angle = frequency_of(lax.broadcasted_iota(i32, (64, TQ), 0)) * pos
        cosine_t = jnp.concatenate([jnp.cos(angle)] * QH, axis=1)
        sine_t = jnp.concatenate([jnp.sin(angle)] * QH, axis=1)
        x1, x2 = back[0:64, :], back[64:128, :]
        turned_back = jnp.concatenate([x1 * cosine_t + x2 * sine_t, x2 * cosine_t - x1 * sine_t], axis=0)
        q_rows = turned_back.T.astype(bf16)
        at_rows = pl.ds(pl.multiple_of(r * TQ, TQ), TQ)
        for h in range(QH):
            dqx[at_rows, 128 * h : 128 * h + 128] = q_rows[TQ * h : TQ * h + TQ, :]
        send_rows(dqx, dq, dq_s, dq_r, r, 8)

    loop(0, ROW_TILES, own_rows)

    for n in range(N_ALL):
        pg[n, 0:4, :] = pkg[4 * n : 4 * n + 4, :]
        pg[n, 4:8, :] = pvg[4 * n : 4 * n + 4, :]

    def prompt_back(n):
        return remote(pg.at[n], pin.at[me_back], pg_s.at[n], pg_r.at[me_back], at_row(n))

    def start_back(n):
        @pl.when(jnp.logical_not(row_is_me(n)))
        def _():
            prompt_back(n).start()

    loop(0, N_ALL, start_back)
    own_back = pltpu.make_async_copy(pg.at[me_in], pin.at[me_back], loc.at[9])

    @pl.when(is_diag)
    def _():
        own_back.start()

    def finish_block(total, j):
        x = total[:, 0:128]
        cosine_j, sine_j = cosines[rows(j * BLOCK), :], sines[rows(j * BLOCK), :]
        own[0, rows(j * BLOCK), :] = (x * cosine_j - pltpu.roll(x, 64, 1) * sine_j).astype(bf16)
        own[1, rows(j * BLOCK), :] = total[:, 128:256].astype(bf16)

    def send_own(k):
        j = lax.rem(c + k, N_CTX)
        mine = dkv[rows(OWN + j * BLOCK), :]

        @pl.when(has_next)
        def _():
            near_copy(j).wait_recv()
            finish_block(mine + near_in[rows(j * BLOCK), :].astype(f32), j)

        @pl.when(jnp.logical_not(has_next))
        def _():
            finish_block(mine, j)

        @pl.when(k < N_CTX)
        def _():
            home(own.at[0], dk, k_s, k_r, 128, j).start()
            home(own.at[1], dv, v_s, v_r, 128, j).start()

    loop(1, N_CTX + 1, send_own)
    home_own(own.at[0], dk, 128, 10).start()
    home_own(own.at[1], dv, 128, 11).start()

    def finish_prompt(n):
        @pl.when(jnp.logical_not(column_is_me(n)))
        def _():
            prompt_copy(n).wait_send()
            remote(pg.at[n], pin.at[n], pg_s.at[n], pg_r.at[n], at_column(n)).wait_recv()

        @pl.when(jnp.logical_not(row_is_me(n)))
        def _():
            prompt_back(n).wait_send()

    loop(0, N_ALL, finish_prompt)

    @pl.when(is_diag)
    def _():
        own_back.wait()

    total = jnp.sum(pin[...], axis=0)
    dpk[...] = total[0:4, :].astype(bf16)
    dpv[...] = total[4:8, :].astype(bf16)

    backs = (
        (ox, out, o_s, o_r, 512),
        (dqx, dq, dq_s, dq_r, 512),
        (own.at[0], dk, k_s, k_r, 128),
        (own.at[1], dv, v_s, v_r, 128),
    )

    def finish(k):
        j = lax.rem(c + k, N_CTX)
        spread(*kv_way, kv_s, kv_r, j).wait_send()
        spread(*d_way, d_s, d_r, j).wait_send()
        spread(*q_way, q_s, q_r, j).wait_send()
        for back in backs:
            home(*back, j).wait_send()
            home_in(*back, j).wait_recv()

    loop(1, N_CTX, finish)
    for at, (src, dst, _, _, width) in zip((7, 8, 10, 11), backs):
        home_own(src, dst, width, at).wait()

    def finish_z(j):
        @pl.when(has_next)
        def _():
            next_copy(j).wait_send()

        @pl.when(middle)
        def _():
            relay_copy(j).wait_send()

        @pl.when(has_far)
        def _():
            far_copy(j).wait_send()

        @pl.when(has_prev)
        def _():
            near_copy(j).wait_send()

    loop(0, N_CTX, finish_z)


def place(*refs):
    sems = refs[-1]
    count = (len(refs) - 1) // 2
    copies = [pltpu.make_async_copy(refs[i], refs[count + i], sems.at[i]) for i in range(count)]
    for copy in copies:
        copy.start()
    for copy in copies:
        copy.wait()


def spec(space):
    return pl.BlockSpec(memory_space=space)


VMEM, SMEM, HBM, ANY = pltpu.VMEM, pltpu.SMEM, pltpu.HBM, pl.ANY
DMA = pltpu.SemaphoreType.DMA


def local(queries, keys_in, values_in, out_grad, lengths, prompt_keys, prompt_values):
    sds = jax.ShapeDtypeStruct
    shapes = (
        sds((BLOCK, 4096), bf16),
        sds((BLOCK, 4096), bf16),
        sds((BLOCK, 1024), bf16),
        sds((BLOCK, 1024), bf16),
        sds((4, 128), bf16),
        sds((4, 128), bf16),
    )
    results = pl.pallas_call(
        step_kernel,
        out_shape=shapes,
        in_specs=[spec(HBM)] * 4 + [spec(SMEM), spec(VMEM), spec(VMEM)],
        out_specs=(spec(VMEM),) * 6,
        scratch_shapes=[
            VMEM((BLOCK, 4096), bf16),
            VMEM((BLOCK, 1024), bf16),
            VMEM((BLOCK, 1024), bf16),
            VMEM((BLOCK, 4096), bf16),
            VMEM((BLOCK, 2048), bf16),
            VMEM((8, 128), f32),
            VMEM((N_ALL, 8, 128), f32),
            VMEM((CHUNK, 512), bf16),
            VMEM((CHUNK, 512), bf16),
            VMEM((WIN, 256), bf16),
            VMEM((WIN, 128), bf16),
            VMEM((ROW_TILES * LANES, 128), bf16),
            VMEM((ROW_TILES * LANES, 128), bf16),
            VMEM((ROW_TILES * LANES, 128), bf16),
            VMEM((128, 128), f32),
            VMEM((128, 128), f32),
            VMEM((HEAD_AT + HEAD_KEYS, LANES), f32),
            VMEM((128, LANES), f32),
            VMEM((ROW_TILES, 128, LANES), f32),
            VMEM((ROW_TILES, 8, LANES), f32),
            VMEM((WIN, 256), f32),
            VMEM((128, 128), f32),
            VMEM((128, 128), f32),
            VMEM((N_ALL, 8, 128), f32),
            VMEM((N_ALL, 8, 128), f32),
            VMEM((CHUNK, 512), bf16),
            VMEM((CHUNK, 512), bf16),
        ]
        + [VMEM((CHUNK, 256), bf16)] * 4
        + [VMEM((2, CHUNK, 128), bf16), VMEM((CHUNK, 128), f32), VMEM((CHUNK, 128), f32)]
        + [DMA((8,))] * 22
        + [DMA((N_ALL,))] * 4
        + [DMA((12,))],
        compiler_params=pltpu.CompilerParams(
            collective_id=0, has_side_effects=True, vmem_limit_bytes=56 << 20
        ),
        name="grpo_step",
    )(queries, out_grad, keys_in, values_in, lengths[0], prompt_keys, prompt_values)
    return pl.pallas_call(
        place,
        out_shape=shapes,
        in_specs=[spec(VMEM)] * 6,
        out_specs=(spec(HBM),) * 6,
        scratch_shapes=[DMA((6,))],
        name="place",
    )(*results)


def solution(mesh):
    tokens = P(("grp", "uly", "ctx"), None)
    prompt = P(("grp", "ctx"), "uly")
    in_specs = (tokens, tokens, tokens, tokens, P("grp", None, None), prompt, prompt)
    out_specs = (tokens, tokens, tokens, tokens, prompt, prompt)
    return jax.shard_map(local, mesh=mesh, in_specs=in_specs, out_specs=out_specs, check_vma=False)
```

```python
import jax
import jax.numpy as jnp
from jax import lax
from jax.experimental import pallas as pl
from jax.experimental.pallas import tpu as pltpu
from jax.sharding import PartitionSpec as P

H = 32
KEY_VALUE_HEADS = 8
HEAD_WIDTH = 128
PROMPT_TOKENS = 128
theta_base = 1000000.0
neg_fill = -1e30

N_GRP, N_ULY, N_CTX = 4, 8, 8
BLOCK = 128
CHUNK = N_CTX * BLOCK
RUN_PLACES = 4
QH = H // KEY_VALUE_HEADS
WIN = 3 * CHUNK
OWN = 2 * CHUNK
TQ = 256
ROW_TILES = CHUNK // TQ
LANES = QH * TQ
STEP = 512
HEAD_KEYS = PROMPT_TOKENS + TQ
HEAD_AT = WIN - TQ
SCALE = HEAD_WIDTH**-0.5
LOG2E = 1.4426950408889634
C2 = SCALE * LOG2E
MESH = pl.DeviceIdType.MESH
f32, bf16, i32 = jnp.float32, jnp.bfloat16, jnp.int32


def frequency_of(index):
    out = jnp.ones(index.shape, f32)
    for bit in range(6):
        power = theta_base ** (-(2.0 * 2**bit) / HEAD_WIDTH)
        out = out * jnp.where((index // 2**bit) % 2 == 1, f32(power), f32(1.0))
    return out


def begins_of(tau, lens):
    l0, l1, l2 = lens
    zero = jnp.zeros_like(tau)
    return (
        jnp.where(tau >= l0, l0, zero)
        + jnp.where(tau >= l0 + l1, l1, zero)
        + jnp.where(tau >= l0 + l1 + l2, l2, zero)
    )


def cos_sin(base, lens):
    tau = base + lax.broadcasted_iota(i32, (BLOCK, HEAD_WIDTH), 0)
    pos = PROMPT_TOKENS + tau - begins_of(tau, lens)
    lane = lax.broadcasted_iota(i32, (BLOCK, HEAD_WIDTH), 1)
    freq = frequency_of(lax.broadcasted_iota(i32, (8, HEAD_WIDTH), 1) % 64)[0:1, :]
    angle = pos.astype(f32) * freq
    sine = jnp.sin(angle)
    return jnp.cos(angle), jnp.where(lane < 64, -sine, sine)


def membership(base, lens, count):
    l0, l1, l2 = lens
    tau = base + lax.broadcasted_iota(i32, (count, HEAD_WIDTH), 0)
    lane = lax.broadcasted_iota(i32, (count, HEAD_WIDTH), 1)
    low = jnp.where(lane == 0, 0, jnp.where(lane == 1, l0, l0 + l1))
    high = jnp.where(lane == 0, l0, jnp.where(lane == 1, l0 + l1, l0 + l1 + l2))
    return (tau >= low) & (tau < high), lane


def dot_nt(a, b):
    return lax.dot_general(a, b, (((1,), (1,)), ((), ())), preferred_element_type=f32)


def dot_nn(a, b):
    return lax.dot_general(a, b, (((1,), (0,)), ((), ())), preferred_element_type=f32)


def dot_tn(a, b):
    return lax.dot_general(a, b, (((0,), (0,)), ((), ())), preferred_element_type=f32)


def step_kernel(
    q_hbm, do_hbm, k_hbm, v_hbm, len_ref, pk_hbm, pv_hbm,
    out, dq, dk, dv, dpk, dpv,
    q_in, k_in, v_in, pk_in, pv_in, qrot, kvs, ptile, pta, rows64, pb, qx, dox, kvw, aug, onehot, qst, dost, kp, vp,
    s_all, o_t, dq_all, stats, dkv, pkg, pvg, pgb, pgin, tot, bin, ft, pfin, ox, dqx,
    far_out, far_in, near_out, near_in, own, cosines, sines,
    q_s, q_r, d_s, d_r, kv_s, kv_r, f_s, f_r, g_s, g_r, o_s, o_r, dq_s, dq_r,
    fo_s, fo_r, no_s, no_r, k_s, k_r, v_s, v_r, p_s, p_r, pb_s, pb_r, pc_s, pc_r, ga_s, ga_r, gb_s, gb_r, gc_s, gc_r, loc,
):
    g, z, c = lax.axis_index("grp"), lax.axis_index("uly"), lax.axis_index("ctx")
    zr = lax.rem(z, RUN_PLACES)
    run = z // RUN_PLACES
    start = zr * CHUNK
    has_next, has_prev = zr < RUN_PLACES - 1, zr > 0
    middle = (zr == 1) | (zr == 2)
    has_far = zr >= 2
    is_diag = z == c
    lens = (len_ref[run, 0], len_ref[run, 1], len_ref[run, 2])
    barrier = pltpu.get_barrier_semaphore()

    def loop(low, high, body):
        def run_body(i, _):
            body(i)
            return 0

        lax.fori_loop(low, high, run_body, 0)

    def rows(at):
        return pl.ds(pl.multiple_of(at, BLOCK), BLOCK)

    def columns(at, width):
        return pl.ds(pl.multiple_of(at * width, width), width)

    def remote(src, dst, s, r, dev):
        return pltpu.make_async_remote_copy(
            src_ref=src, dst_ref=dst, send_sem=s, recv_sem=r, device_id=dev, device_id_type=MESH
        )

    load_k = pltpu.make_async_copy(k_hbm, k_in, loc.at[0])
    load_v = pltpu.make_async_copy(v_hbm, v_in, loc.at[1])
    load_q = pltpu.make_async_copy(q_hbm, q_in, loc.at[2])
    load_k.start()
    load_v.start()
    load_q.start()
    load_pk = pltpu.make_async_copy(pk_hbm, pk_in, loc.at[12])
    load_pv = pltpu.make_async_copy(pv_hbm, pv_in, loc.at[13])
    load_pk.start()
    load_pv.start()

    def greet(dev):
        pl.semaphore_signal(barrier, inc=1, device_id=dev, device_id_type=MESH)

    loop(1, N_CTX, lambda k: greet((g, z, lax.rem(c + k, N_CTX))))

    @pl.when(has_prev)
    def _():
        greet((g, z - 1, c))

    @pl.when(has_next)
    def _():
        greet((g, z + 1, c))

    hub = (g, c, c)

    @pl.when(is_diag)
    def _():
        loop(1, N_ULY, lambda k: greet((g, lax.rem(z + k, N_ULY), c)))
        loop(1, N_GRP, lambda k: greet((lax.rem(g + k, N_GRP), z, c)))

    @pl.when(jnp.logical_not(is_diag))
    def _():
        greet(hub)

    cosine, sine = cos_sin(start + c * BLOCK, lens)

    def turned(block):
        x = block.astype(f32)
        return (x * cosine + pltpu.roll(x, 64, 1) * sine).astype(bf16)

    load_k.wait()
    load_v.wait()
    for j in range(KEY_VALUE_HEADS):
        kvs[:, 256 * j : 256 * j + 128] = turned(k_in[:, 128 * j : 128 * j + 128])
        kvs[:, 256 * j + 128 : 256 * j + 256] = v_in[:, 128 * j : 128 * j + 128]
    load_pk.wait()
    load_pv.wait()
    ptile[0:4, :] = pk_in[...].astype(f32)
    ptile[4:8, :] = pv_in[...].astype(f32)

    pl.semaphore_wait(
        barrier,
        (N_CTX - 1)
        + jnp.where(has_next, 1, 0)
        + jnp.where(has_prev, 1, 0)
        + jnp.where(is_diag, N_ULY - 1 + N_GRP - 1, 1),
    )

    def spread(src, width, dst, base, s, r, peer):
        return remote(
            src.at[:, columns(peer, width)], dst.at[rows(base + c * BLOCK), :],
            s.at[peer], r.at[c], (g, z, peer),
        )

    def spread_in(src, width, dst, base, s, r, j):
        return remote(
            src.at[:, columns(j, width)], dst.at[rows(base + j * BLOCK), :], s.at[j], r.at[j], (g, z, j)
        )

    def spread_own(src, width, dst, base, at):
        return pltpu.make_async_copy(
            src.at[:, columns(c, width)], dst.at[rows(base + c * BLOCK), :], loc.at[at]
        )

    kv_way = (kvs, 256, kvw, OWN)
    d_way = (do_hbm, 512, dox, 0)
    q_way = (qrot, 512, qx, 0)
    loop(1, N_CTX, lambda k: spread(*kv_way, kv_s, kv_r, lax.rem(c + k, N_CTX)).start())
    spread_own(*kv_way, 3).start()

    def tile_copy(at):
        return remote(ptile, pta.at[at], p_s.at[0], p_r.at[at], (g, z, z))

    def group_copy(at, k):
        return remote(pb.at[at], pb.at[at], pb_s.at[k], pb_r.at[at], (lax.rem(g + k, N_GRP), z, c))

    def column_copy(k):
        return remote(pb, pb, pc_s.at[k], pc_r.at[0], (g, lax.rem(z + k, N_ULY), c))

    @pl.when(is_diag)
    def _():
        pta[c] = ptile[...]

    @pl.when(jnp.logical_not(is_diag))
    def _():
        tile_copy(c).start()

    load_q.wait()

    def turn_heads(peer):
        for h in range(QH):
            at = columns(peer * QH + h, 128)
            qrot[:, at] = turned(q_in[:, at])

    def start_q(k):
        peer = lax.rem(c + k, N_CTX)
        turn_heads(peer)
        spread(*q_way, q_s, q_r, peer).start()

    loop(1, N_CTX, start_q)
    turn_heads(c)
    spread_own(*q_way, 6).start()

    @pl.when(is_diag)
    def _():
        loop(1, N_CTX, lambda k: tile_copy(lax.rem(c + k, N_CTX)).wait_recv())
        for n in range(N_CTX):
            rows64[4 * n : 4 * n + 4, :] = pta[n, 0:4, :]
            rows64[32 + 4 * n : 36 + 4 * n, :] = pta[n, 4:8, :]
        pb[g] = rows64[...].astype(bf16)
        loop(1, N_GRP, lambda k: group_copy(g, k).start())

    above = jnp.where(has_next, z + 1, z - 1)
    below = jnp.where(has_prev, z - 1, z + 1)

    def next_copy(j):
        return remote(
            kvw.at[rows(OWN + j * BLOCK), :], kvw.at[rows(CHUNK + j * BLOCK), :],
            f_s.at[j], f_r.at[j], (g, above, c),
        )

    def relay_copy(j):
        return remote(
            kvw.at[rows(CHUNK + j * BLOCK), :], kvw.at[rows(j * BLOCK), :],
            g_s.at[j], g_r.at[j], (g, above, c),
        )

    spread_own(*kv_way, 3).wait()

    @pl.when(has_next)
    def _():
        next_copy(c).start()

    def pass_on(k):
        j = lax.rem(c + N_CTX - k, N_CTX)
        spread_in(*kv_way, kv_s, kv_r, j).wait_recv()

        @pl.when(has_next)
        def _():
            next_copy(j).start()

    loop(1, N_CTX, pass_on)
    loop(1, N_CTX, lambda k: spread(*d_way, d_s, d_r, lax.rem(c + k, N_CTX)).start())
    spread_own(*d_way, 5).start()

    @pl.when(is_diag)
    def _():
        loop(1, N_GRP, lambda k: group_copy(lax.rem(g + k, N_GRP), k).wait_recv())
        loop(1, N_ULY, lambda k: column_copy(k).start())

    def tables(j):
        cosine_j, sine_j = cos_sin(start + j * BLOCK, lens)
        cosines[rows(j * BLOCK), :] = cosine_j
        sines[rows(j * BLOCK), :] = sine_j

    loop(0, N_CTX, tables)

    def key_masks(j):
        inside, lane = membership(start + j * BLOCK - OWN, lens, BLOCK)
        aug[rows(j * BLOCK), :] = jnp.where(inside | (lane >= 3), 0.0, neg_fill).astype(bf16)

    loop(0, WIN // BLOCK, key_masks)

    def query_masks(r):
        inside, lane = membership(start + r * TQ, lens, TQ)
        hot = jnp.where(inside & (lane < 3), 1.0, 0.0).astype(bf16)
        for h in range(QH):
            onehot[pl.ds(pl.multiple_of(r * LANES + h * TQ, TQ), TQ), :] = hot

    loop(0, ROW_TILES, query_masks)
    def clear(j):
        dkv[rows(j * BLOCK), :] = jnp.zeros((BLOCK, 256), f32)

    loop(0, WIN // BLOCK, clear)

    def pass_far(k):
        j = lax.rem(k + 4, N_CTX)

        @pl.when(has_prev)
        def _():
            next_copy(j).wait_recv()

        @pl.when(middle)
        def _():
            relay_copy(j).start()

    loop(0, N_CTX, pass_far)
    spread_own(*q_way, 6).wait()

    @pl.when(jnp.logical_not(is_diag))
    def _():
        column_copy(1).wait_recv()

    for n in range(N_GRP):
        kp[32 * n : 32 * n + 32, :] = pb[n, 0:32, :]
        vp[32 * n : 32 * n + 32, :] = pb[n, 32:64, :]

    def keys_at(at, count):
        return pl.ds(pl.multiple_of(at, 256), count)

    def tile_rows(r):
        return pl.ds(pl.multiple_of(r * LANES, LANES), LANES)

    def masked_queries(r):
        return jnp.concatenate([onehot[tile_rows(r), :], qst[tile_rows(r), :]], axis=1)

    def masked_keys(at, count):
        return jnp.concatenate([aug[keys_at(at, count), :], kvw[keys_at(at, count), 0:128]], axis=1)

    def head_keys(r):
        first = jnp.concatenate([jnp.zeros((PROMPT_TOKENS, 128), bf16), kp[...]], axis=1)
        return jnp.concatenate([first, masked_keys(OWN + r * TQ, TQ)], axis=0)

    def head_values(r):
        return jnp.concatenate([vp[...], kvw[keys_at(OWN + r * TQ, TQ), 128:256]], axis=0)

    def head_scores(r, qa):
        s = dot_nt(head_keys(r), qa)
        key = lax.broadcasted_iota(i32, (HEAD_KEYS, LANES), 0) - PROMPT_TOKENS
        token = lax.broadcasted_iota(i32, (HEAD_KEYS, LANES), 1) % TQ
        return jnp.where(key <= token, s, neg_fill)

    head_at = pl.ds(HEAD_AT, HEAD_KEYS)

    def first_step(r):
        return jnp.where(has_far, r // 2, jnp.where(has_prev, CHUNK // STEP, OWN // STEP))

    def forward(k):
        r = ROW_TILES - 1 - k

        for e in range(2):
            j = 2 * r + e

            @pl.when(j != c)
            def _():
                spread_in(*q_way, q_s, q_r, j).wait_recv()

        at_rows = pl.ds(pl.multiple_of(r * TQ, TQ), TQ)
        for h in range(QH):
            to = pl.ds(pl.multiple_of(r * LANES + h * TQ, TQ), TQ)
            qst[to, :] = qx[at_rows, 128 * h : 128 * h + 128]
        qa = masked_queries(r)
        low = first_step(r)

        s = head_scores(r, qa)
        s_all[head_at, :] = s
        top = jnp.max(s, axis=0, keepdims=True)

        def score(at, count, top):
            s = dot_nt(masked_keys(at, count), qa)
            s_all[keys_at(at, count), :] = s
            return jnp.maximum(top, jnp.max(s, axis=0, keepdims=True))

        top = lax.fori_loop(0, r, lambda t, a: score(OWN + t * TQ, TQ, a), top)
        near_low = jnp.where(has_prev, CHUNK // STEP, OWN // STEP)
        top = lax.fori_loop(near_low, OWN // STEP, lambda t, a: score(t * STEP, STEP, a), top)

        @pl.when(has_far & (lax.rem(k, 2) == 0))
        def _():
            loop(0, 4, lambda j: relay_copy(4 - 2 * k + j).wait_recv())

        top = lax.fori_loop(low, near_low, lambda t, a: score(t * STEP, STEP, a), top)
        top = top * C2

        def power(at, total):
            p = jnp.exp2(s_all[at, :] * C2 - top)
            s_all[at, :] = p
            return total + jnp.sum(p, axis=0, keepdims=True)

        total = power(head_at, jnp.zeros((1, LANES), f32))
        total = lax.fori_loop(0, r, lambda t, a: power(keys_at(OWN + t * TQ, TQ), a), total)
        total = lax.fori_loop(low, OWN // STEP, lambda t, a: power(keys_at(t * STEP, STEP), a), total)
        inverse = 1.0 / total
        o_t[...] = dot_tn(head_values(r), (s_all[head_at, :] * inverse).astype(bf16))

        def gather(at, count):
            half = (s_all[keys_at(at, count), :] * inverse).astype(bf16)
            o_t[...] += dot_tn(kvw[keys_at(at, count), 128:256], half)

        loop(0, r, lambda t: gather(OWN + t * TQ, TQ))
        loop(low, OWN // STEP, lambda t: gather(t * STEP, STEP))
        for e in range(2):
            j = 2 * r + e

            @pl.when(j != c)
            def _():
                spread_in(*d_way, d_s, d_r, j).wait_recv()

            @pl.when(j == c)
            def _():
                spread_own(*d_way, 5).wait()

        for h in range(QH):
            to = pl.ds(pl.multiple_of(r * LANES + h * TQ, TQ), TQ)
            dost[to, :] = dox[at_rows, 128 * h : 128 * h + 128]
        o = o_t[...].astype(bf16).astype(f32)
        delta = jnp.sum(o * dost[tile_rows(r), :].astype(f32).T, axis=0, keepdims=True)
        stats[r, 0:1, :] = top + jnp.log(total) * LOG2E
        stats[r, 1:2, :] = delta
        o_rows = o.T.astype(bf16)
        for h in range(QH):
            ox[at_rows, 128 * h : 128 * h + 128] = o_rows[TQ * h : TQ * h + TQ, :]
        send_rows(ox, out, o_s, o_r, r, 7)

    def home(src, dst, s, r, width, peer):
        return remote(
            src.at[rows(peer * BLOCK), :], dst.at[:, columns(c, width)], s.at[peer], r.at[c], (g, z, peer)
        )

    def home_in(src, dst, s, r, width, j):
        return remote(
            src.at[rows(j * BLOCK), :], dst.at[:, columns(j, width)], s.at[j], r.at[j], (g, z, j)
        )

    def home_own(src, dst, width, at):
        return pltpu.make_async_copy(src.at[rows(c * BLOCK), :], dst.at[:, columns(c, width)], loc.at[at])

    def send_rows(src, dst, s, rs, r, at):
        for e in range(2):
            j = 2 * r + e

            @pl.when(j != c)
            def _():
                home(src, dst, s, rs, 512, j).start()

            @pl.when(j == c)
            def _():
                home_own(src, dst, 512, at).start()

    loop(0, ROW_TILES, forward)

    def grads(r, s, v):
        p = jnp.exp2(s * C2 - stats[r, 0:1, :])
        dp = dot_nt(v, dost[tile_rows(r), :])
        ds = (p * (dp - stats[r, 1:2, :]) * SCALE).astype(bf16)
        return p.astype(bf16), ds

    def backward(r, at, count):
        s = dot_nt(masked_keys(at, count), masked_queries(r))
        here = keys_at(at, count)
        half, ds = grads(r, s, kvw[here, 128:256])
        dq_all[r] += dot_tn(kvw[here, 0:128], ds)
        dkv[here, 0:128] += dot_nn(ds, qst[tile_rows(r), :])
        dkv[here, 128:256] += dot_nn(half, dost[tile_rows(r), :])

    pkg[...] = jnp.zeros((128, 128), f32)
    pvg[...] = jnp.zeros((128, 128), f32)

    def prompt_rows(r):
        half, ds = grads(r, dot_nt(kp[...], qst[tile_rows(r), :]), vp[...])
        dq_all[r] = dot_tn(kp[...], ds)
        pkg[...] += dot_nn(ds, qst[tile_rows(r), :])
        pvg[...] += dot_nn(half, dost[tile_rows(r), :])

    loop(0, ROW_TILES, prompt_rows)
    for n in range(N_GRP):
        pgb[n, 0:32, :] = pkg[32 * n : 32 * n + 32, :].astype(bf16)
        pgb[n, 32:64, :] = pvg[32 * n : 32 * n + 32, :].astype(bf16)

    def to_hub(at):
        return remote(pgb, pgin.at[at], ga_s.at[0], ga_r.at[at], hub)

    def over_groups(at, k):
        gg = lax.rem(g + k, N_GRP)
        return remote(tot.at[gg], bin.at[at], gb_s.at[k], gb_r.at[at], (gg, z, c))

    def to_owner(k):
        cc = lax.rem(c + k, N_CTX)
        return remote(ft.at[cc], pfin, gc_s.at[k], gc_r.at[0], (g, z, cc))

    @pl.when(is_diag)
    def _():
        pgin[z] = pgb[...]

    @pl.when(jnp.logical_not(is_diag))
    def _():
        to_hub(z).start()

    def far_copy(j):
        return remote(
            far_out.at[rows(j * BLOCK), :], far_in.at[rows(j * BLOCK), :], fo_s.at[j], fo_r.at[j], (g, below, c)
        )

    def near_copy(j):
        return remote(
            near_out.at[rows(j * BLOCK), :], near_in.at[rows(j * BLOCK), :], no_s.at[j], no_r.at[j], (g, below, c)
        )

    def send_far(j):
        far_out[rows(j * BLOCK), :] = dkv[rows(j * BLOCK), :].astype(bf16)
        far_copy(j).start()

    blocks = STEP // BLOCK

    @pl.when(has_far)
    def _():
        def far_keys(t):
            loop(0, 2 + 2 * t, lambda r: backward(r, t * STEP, STEP))
            loop(blocks * t, blocks * t + blocks, send_far)

        loop(0, CHUNK // STEP, far_keys)

    @pl.when(is_diag)
    def _():
        loop(1, N_ULY, lambda k: to_hub(lax.rem(z + k, N_ULY)).wait_recv())
        for n in range(N_GRP):
            part = pgin[0, n].astype(f32)
            for m in range(1, N_ULY):
                part = part + pgin[m, n].astype(f32)
            tot[n] = part
        bin[g] = tot[g]

    def send_near(j):
        mine = dkv[rows(CHUNK + j * BLOCK), :]

        @pl.when(middle)
        def _():
            far_copy(j).wait_recv()
            near_out[rows(j * BLOCK), :] = (mine + far_in[rows(j * BLOCK), :].astype(f32)).astype(bf16)

        @pl.when(jnp.logical_not(middle))
        def _():
            near_out[rows(j * BLOCK), :] = mine.astype(bf16)

        near_copy(j).start()

    @pl.when(has_prev)
    def _():
        def near_keys(t):
            loop(0, ROW_TILES, lambda r: backward(r, CHUNK + t * STEP, STEP))
            loop(blocks * t, blocks * t + blocks, send_near)

        loop(0, CHUNK // STEP, near_keys)

    @pl.when(is_diag)
    def _():
        loop(1, N_GRP, lambda k: over_groups(g, k).start())

    def own_rows(k):
        r = lax.rem(c // 2 + k, ROW_TILES)
        loop(0, r, lambda t: backward(r, OWN + t * TQ, TQ))
        here = keys_at(OWN + r * TQ, TQ)
        s = dot_nt(masked_keys(OWN + r * TQ, TQ), masked_queries(r))
        key = lax.broadcasted_iota(i32, (TQ, LANES), 0)
        token = lax.broadcasted_iota(i32, (TQ, LANES), 1) % TQ
        half, ds = grads(r, jnp.where(key <= token, s, neg_fill), kvw[here, 128:256])
        back = dq_all[r] + dot_tn(kvw[here, 0:128], ds)
        dkv[here, 0:128] += dot_nn(ds, qst[tile_rows(r), :])
        dkv[here, 128:256] += dot_nn(half, dost[tile_rows(r), :])
        tau = start + r * TQ + lax.broadcasted_iota(i32, (1, TQ), 1)
        pos = (PROMPT_TOKENS + tau - begins_of(tau, lens)).astype(f32)
        angle = frequency_of(lax.broadcasted_iota(i32, (64, TQ), 0)) * pos
        cosine_t = jnp.concatenate([jnp.cos(angle)] * QH, axis=1)
        sine_t = jnp.concatenate([jnp.sin(angle)] * QH, axis=1)
        x1, x2 = back[0:64, :], back[64:128, :]
        turned_back = jnp.concatenate([x1 * cosine_t + x2 * sine_t, x2 * cosine_t - x1 * sine_t], axis=0)
        q_rows = turned_back.T.astype(bf16)
        at_rows = pl.ds(pl.multiple_of(r * TQ, TQ), TQ)
        for h in range(QH):
            dqx[at_rows, 128 * h : 128 * h + 128] = q_rows[TQ * h : TQ * h + TQ, :]
        send_rows(dqx, dq, dq_s, dq_r, r, 8)

    loop(0, ROW_TILES, own_rows)

    def finish_block(total, j):
        x = total[:, 0:128]
        cosine_j, sine_j = cosines[rows(j * BLOCK), :], sines[rows(j * BLOCK), :]
        own[0, rows(j * BLOCK), :] = (x * cosine_j - pltpu.roll(x, 64, 1) * sine_j).astype(bf16)
        own[1, rows(j * BLOCK), :] = total[:, 128:256].astype(bf16)

    def send_own(k):
        j = lax.rem(c + k, N_CTX)
        mine = dkv[rows(OWN + j * BLOCK), :]

        @pl.when(has_next)
        def _():
            near_copy(j).wait_recv()
            finish_block(mine + near_in[rows(j * BLOCK), :].astype(f32), j)

        @pl.when(jnp.logical_not(has_next))
        def _():
            finish_block(mine, j)

        @pl.when(k < N_CTX)
        def _():
            home(own.at[0], dk, k_s, k_r, 128, j).start()
            home(own.at[1], dv, v_s, v_r, 128, j).start()

    loop(1, N_CTX + 1, send_own)
    home_own(own.at[0], dk, 128, 10).start()
    home_own(own.at[1], dv, 128, 11).start()

    @pl.when(is_diag)
    def _():
        loop(1, N_GRP, lambda k: over_groups(lax.rem(g + k, N_GRP), k).wait_recv())
        whole = bin[0] + bin[1] + bin[2] + bin[3]
        for n in range(N_CTX):
            ft[n, 0:4, :] = whole[4 * n : 4 * n + 4, :]
            ft[n, 4:8, :] = whole[32 + 4 * n : 36 + 4 * n, :]
        loop(1, N_CTX, lambda k: to_owner(k).start())
        pfin[...] = ft[c]

    @pl.when(is_diag)
    def _():
        loop(1, N_GRP, lambda k: group_copy(g, k).wait_send())
        loop(1, N_ULY, lambda k: column_copy(k).wait_send())
        loop(1, N_GRP, lambda k: over_groups(g, k).wait_send())
        loop(1, N_CTX, lambda k: to_owner(k).wait_send())

    @pl.when(jnp.logical_not(is_diag))
    def _():
        tile_copy(c).wait_send()
        to_hub(z).wait_send()
        to_owner(1).wait_recv()

    total = pfin[...]
    dpk[...] = total[0:4, :].astype(bf16)
    dpv[...] = total[4:8, :].astype(bf16)

    backs = (
        (ox, out, o_s, o_r, 512),
        (dqx, dq, dq_s, dq_r, 512),
        (own.at[0], dk, k_s, k_r, 128),
        (own.at[1], dv, v_s, v_r, 128),
    )

    def finish(k):
        j = lax.rem(c + k, N_CTX)
        spread(*kv_way, kv_s, kv_r, j).wait_send()
        spread(*d_way, d_s, d_r, j).wait_send()
        spread(*q_way, q_s, q_r, j).wait_send()
        for back in backs:
            home(*back, j).wait_send()
            home_in(*back, j).wait_recv()

    loop(1, N_CTX, finish)
    for at, (src, dst, _, _, width) in zip((7, 8, 10, 11), backs):
        home_own(src, dst, width, at).wait()

    def finish_z(j):
        @pl.when(has_next)
        def _():
            next_copy(j).wait_send()

        @pl.when(middle)
        def _():
            relay_copy(j).wait_send()

        @pl.when(has_far)
        def _():
            far_copy(j).wait_send()

        @pl.when(has_prev)
        def _():
            near_copy(j).wait_send()

    loop(0, N_CTX, finish_z)


def place(*refs):
    sems = refs[-1]
    count = (len(refs) - 1) // 2
    copies = [pltpu.make_async_copy(refs[i], refs[count + i], sems.at[i]) for i in range(count)]
    for copy in copies:
        copy.start()
    for copy in copies:
        copy.wait()


def spec(space):
    return pl.BlockSpec(memory_space=space)


VMEM, SMEM, HBM, ANY = pltpu.VMEM, pltpu.SMEM, pltpu.HBM, pl.ANY
DMA = pltpu.SemaphoreType.DMA


def local(queries, keys_in, values_in, out_grad, lengths, prompt_keys, prompt_values):
    sds = jax.ShapeDtypeStruct
    shapes = (
        sds((BLOCK, 4096), bf16),
        sds((BLOCK, 4096), bf16),
        sds((BLOCK, 1024), bf16),
        sds((BLOCK, 1024), bf16),
        sds((4, 128), bf16),
        sds((4, 128), bf16),
    )
    results = pl.pallas_call(
        step_kernel,
        out_shape=shapes,
        in_specs=[spec(HBM)] * 4 + [spec(SMEM), spec(HBM), spec(HBM)],
        out_specs=(spec(VMEM),) * 6,
        scratch_shapes=[
            VMEM((BLOCK, 4096), bf16),
            VMEM((BLOCK, 1024), bf16),
            VMEM((BLOCK, 1024), bf16),
            VMEM((4, 128), bf16),
            VMEM((4, 128), bf16),
            VMEM((BLOCK, 4096), bf16),
            VMEM((BLOCK, 2048), bf16),
            VMEM((8, 128), f32),
            VMEM((N_CTX, 8, 128), f32),
            VMEM((64, 128), f32),
            VMEM((N_GRP, 64, 128), bf16),
            VMEM((CHUNK, 512), bf16),
            VMEM((CHUNK, 512), bf16),
            VMEM((WIN, 256), bf16),
            VMEM((WIN, 128), bf16),
            VMEM((ROW_TILES * LANES, 128), bf16),
            VMEM((ROW_TILES * LANES, 128), bf16),
            VMEM((ROW_TILES * LANES, 128), bf16),
            VMEM((128, 128), bf16),
            VMEM((128, 128), bf16),
            VMEM((HEAD_AT + HEAD_KEYS, LANES), f32),
            VMEM((128, LANES), f32),
            VMEM((ROW_TILES, 128, LANES), f32),
            VMEM((ROW_TILES, 8, LANES), f32),
            VMEM((WIN, 256), f32),
            VMEM((128, 128), f32),
            VMEM((128, 128), f32),
            VMEM((N_GRP, 64, 128), bf16),
            VMEM((N_ULY, N_GRP, 64, 128), bf16),
            VMEM((N_GRP, 64, 128), f32),
            VMEM((N_GRP, 64, 128), f32),
            VMEM((N_CTX, 8, 128), f32),
            VMEM((8, 128), f32),
            VMEM((CHUNK, 512), bf16),
            VMEM((CHUNK, 512), bf16),
        ]
        + [VMEM((CHUNK, 256), bf16)] * 4
        + [VMEM((2, CHUNK, 128), bf16), VMEM((CHUNK, 128), f32), VMEM((CHUNK, 128), f32)]
        + [DMA((8,))] * 22
        + [DMA((8,))] * 12
        + [DMA((14,))],
        compiler_params=pltpu.CompilerParams(
            collective_id=0, has_side_effects=True, vmem_limit_bytes=56 << 20
        ),
        name="grpo_step",
    )(queries, out_grad, keys_in, values_in, lengths[0], prompt_keys, prompt_values)
    return pl.pallas_call(
        place,
        out_shape=shapes,
        in_specs=[spec(VMEM)] * 6,
        out_specs=(spec(HBM),) * 6,
        scratch_shapes=[DMA((6,))],
        name="place",
    )(*results)


def solution(mesh):
    tokens = P(("grp", "uly", "ctx"), None)
    prompt = P(("grp", "ctx"), "uly")
    in_specs = (tokens, tokens, tokens, tokens, P("grp", None, None), prompt, prompt)
    out_specs = (tokens, tokens, tokens, tokens, prompt, prompt)
    return jax.shard_map(local, mesh=mesh, in_specs=in_specs, out_specs=out_specs, check_vma=False)
```

```python
import jax
import jax.numpy as jnp
from jax import lax
from jax.experimental import pallas as pl
from jax.experimental.pallas import tpu as pltpu
from jax.sharding import PartitionSpec as P

H = 32
KEY_VALUE_HEADS = 8
HEAD_WIDTH = 128
PROMPT_TOKENS = 128
theta_base = 1000000.0
neg_fill = -1e30

N_GRP, N_ULY, N_CTX = 4, 8, 8
BLOCK = 128
CHUNK = N_CTX * BLOCK
RUN_PLACES = 4
QH = H // KEY_VALUE_HEADS
WIN = 3 * CHUNK
OWN = 2 * CHUNK
TQ = 256
ROW_TILES = CHUNK // TQ
LANES = QH * TQ
STEP = 512
HEAD_KEYS = PROMPT_TOKENS + TQ
HEAD_AT = WIN - TQ
SCALE = HEAD_WIDTH**-0.5
LOG2E = 1.4426950408889634
C2 = SCALE * LOG2E
MESH = pl.DeviceIdType.MESH
f32, bf16, i32 = jnp.float32, jnp.bfloat16, jnp.int32


def frequency_of(index):
    out = jnp.ones(index.shape, f32)
    for bit in range(6):
        power = theta_base ** (-(2.0 * 2**bit) / HEAD_WIDTH)
        out = out * jnp.where((index // 2**bit) % 2 == 1, f32(power), f32(1.0))
    return out


def begins_of(tau, lens):
    l0, l1, l2 = lens
    zero = jnp.zeros_like(tau)
    return (
        jnp.where(tau >= l0, l0, zero)
        + jnp.where(tau >= l0 + l1, l1, zero)
        + jnp.where(tau >= l0 + l1 + l2, l2, zero)
    )


def cos_sin(base, lens):
    tau = base + lax.broadcasted_iota(i32, (BLOCK, HEAD_WIDTH), 0)
    pos = PROMPT_TOKENS + tau - begins_of(tau, lens)
    lane = lax.broadcasted_iota(i32, (BLOCK, HEAD_WIDTH), 1)
    freq = frequency_of(lax.broadcasted_iota(i32, (8, HEAD_WIDTH), 1) % 64)[0:1, :]
    angle = pos.astype(f32) * freq
    sine = jnp.sin(angle)
    return jnp.cos(angle), jnp.where(lane < 64, -sine, sine)


def membership(base, lens, count):
    l0, l1, l2 = lens
    tau = base + lax.broadcasted_iota(i32, (count, HEAD_WIDTH), 0)
    lane = lax.broadcasted_iota(i32, (count, HEAD_WIDTH), 1)
    low = jnp.where(lane == 0, 0, jnp.where(lane == 1, l0, l0 + l1))
    high = jnp.where(lane == 0, l0, jnp.where(lane == 1, l0 + l1, l0 + l1 + l2))
    return (tau >= low) & (tau < high), lane


def dot_nt(a, b):
    return lax.dot_general(a, b, (((1,), (1,)), ((), ())), preferred_element_type=f32)


def dot_nn(a, b):
    return lax.dot_general(a, b, (((1,), (0,)), ((), ())), preferred_element_type=f32)


def dot_tn(a, b):
    return lax.dot_general(a, b, (((0,), (0,)), ((), ())), preferred_element_type=f32)


def step_kernel(
    q_hbm, do_hbm, k_hbm, v_hbm, len_ref, pk_hbm, pv_hbm,
    out, dq, dk, dv, dpk, dpv,
    q_in, k_in, v_in, pk_in, pv_in, qrot, kvs, ptile, pta, rows64, pb, qx, dox, kvw, aug, onehot, qst, dost, kp, vp,
    s_all, o_t, dq_all, stats, dkv, pkg, pvg, pgb, pgin, tot, bin, ft, pfin, ox, dqx,
    far_out, far_in, near_out, near_in, own, cosines, sines,
    q_s, q_r, d_s, d_r, kv_s, kv_r, f_s, f_r, g_s, g_r, o_s, o_r, dq_s, dq_r,
    fo_s, fo_r, no_s, no_r, k_s, k_r, v_s, v_r, p_s, p_r, pb_s, pb_r, pc_s, pc_r, ga_s, ga_r, gb_s, gb_r, gc_s, gc_r, loc,
):
    g, z, c = lax.axis_index("grp"), lax.axis_index("uly"), lax.axis_index("ctx")
    zr = lax.rem(z, RUN_PLACES)
    run = z // RUN_PLACES
    start = zr * CHUNK
    has_next, has_prev = zr < RUN_PLACES - 1, zr > 0
    middle = (zr == 1) | (zr == 2)
    has_far = zr >= 2
    is_diag = z == c
    lens = (len_ref[run, 0], len_ref[run, 1], len_ref[run, 2])
    barrier = pltpu.get_barrier_semaphore()

    def loop(low, high, body):
        def run_body(i, _):
            body(i)
            return 0

        lax.fori_loop(low, high, run_body, 0)

    def rows(at):
        return pl.ds(pl.multiple_of(at, BLOCK), BLOCK)

    def columns(at, width):
        return pl.ds(pl.multiple_of(at * width, width), width)

    def remote(src, dst, s, r, dev):
        return pltpu.make_async_remote_copy(
            src_ref=src, dst_ref=dst, send_sem=s, recv_sem=r, device_id=dev, device_id_type=MESH
        )

    load_k = pltpu.make_async_copy(k_hbm, k_in, loc.at[0])
    load_v = pltpu.make_async_copy(v_hbm, v_in, loc.at[1])
    load_q = pltpu.make_async_copy(q_hbm, q_in, loc.at[2])
    load_k.start()
    load_v.start()
    load_q.start()
    load_pk = pltpu.make_async_copy(pk_hbm, pk_in, loc.at[12])
    load_pv = pltpu.make_async_copy(pv_hbm, pv_in, loc.at[13])
    load_pk.start()
    load_pv.start()

    def greet(dev):
        pl.semaphore_signal(barrier, inc=1, device_id=dev, device_id_type=MESH)

    loop(1, N_CTX, lambda k: greet((g, z, lax.rem(c + k, N_CTX))))

    @pl.when(has_prev)
    def _():
        greet((g, z - 1, c))

    @pl.when(has_next)
    def _():
        greet((g, z + 1, c))

    hub = (g, c, c)

    @pl.when(is_diag)
    def _():
        loop(1, N_ULY, lambda k: greet((g, lax.rem(z + k, N_ULY), c)))
        loop(1, N_GRP, lambda k: greet((lax.rem(g + k, N_GRP), z, c)))

    @pl.when(jnp.logical_not(is_diag))
    def _():
        greet(hub)

    cosine, sine = cos_sin(start + c * BLOCK, lens)

    def turned(block):
        x = block.astype(f32)
        return (x * cosine + pltpu.roll(x, 64, 1) * sine).astype(bf16)

    load_k.wait()
    load_v.wait()
    for j in range(KEY_VALUE_HEADS):
        kvs[:, 256 * j : 256 * j + 128] = turned(k_in[:, 128 * j : 128 * j + 128])
        kvs[:, 256 * j + 128 : 256 * j + 256] = v_in[:, 128 * j : 128 * j + 128]
    load_pk.wait()
    load_pv.wait()
    ptile[0:4, :] = pk_in[...].astype(f32)
    ptile[4:8, :] = pv_in[...].astype(f32)

    pl.semaphore_wait(
        barrier,
        (N_CTX - 1)
        + jnp.where(has_next, 1, 0)
        + jnp.where(has_prev, 1, 0)
        + jnp.where(is_diag, N_ULY - 1 + N_GRP - 1, 1),
    )

    def spread(src, width, dst, base, s, r, peer):
        return remote(
            src.at[:, columns(peer, width)], dst.at[rows(base + c * BLOCK), :],
            s.at[peer], r.at[c], (g, z, peer),
        )

    def spread_in(src, width, dst, base, s, r, j):
        return remote(
            src.at[:, columns(j, width)], dst.at[rows(base + j * BLOCK), :], s.at[j], r.at[j], (g, z, j)
        )

    def spread_own(src, width, dst, base, at):
        return pltpu.make_async_copy(
            src.at[:, columns(c, width)], dst.at[rows(base + c * BLOCK), :], loc.at[at]
        )

    kv_way = (kvs, 256, kvw, OWN)
    d_way = (do_hbm, 512, dox, 0)
    q_way = (qrot, 512, qx, 0)
    loop(1, N_CTX, lambda k: spread(*kv_way, kv_s, kv_r, lax.rem(c + k, N_CTX)).start())
    spread_own(*kv_way, 3).start()

    def tile_copy(at):
        return remote(ptile, pta.at[at], p_s.at[0], p_r.at[at], (g, z, z))

    def group_copy(at, k):
        return remote(pb.at[at], pb.at[at], pb_s.at[k], pb_r.at[at], (lax.rem(g + k, N_GRP), z, c))

    def column_copy(k):
        return remote(pb, pb, pc_s.at[k], pc_r.at[0], (g, lax.rem(z + k, N_ULY), c))

    @pl.when(is_diag)
    def _():
        pta[c] = ptile[...]

    @pl.when(jnp.logical_not(is_diag))
    def _():
        tile_copy(c).start()

    load_q.wait()

    def turn_heads(peer):
        for h in range(QH):
            at = columns(peer * QH + h, 128)
            qrot[:, at] = turned(q_in[:, at])

    def start_q(k):
        peer = lax.rem(c + k, N_CTX)
        turn_heads(peer)
        spread(*q_way, q_s, q_r, peer).start()

    loop(1, N_CTX, start_q)
    turn_heads(c)
    spread_own(*q_way, 6).start()

    @pl.when(is_diag)
    def _():
        loop(1, N_CTX, lambda k: tile_copy(lax.rem(c + k, N_CTX)).wait_recv())
        for n in range(N_CTX):
            rows64[4 * n : 4 * n + 4, :] = pta[n, 0:4, :]
            rows64[32 + 4 * n : 36 + 4 * n, :] = pta[n, 4:8, :]
        pb[g] = rows64[...].astype(bf16)
        loop(1, N_GRP, lambda k: group_copy(g, k).start())

    above = jnp.where(has_next, z + 1, z - 1)
    below = jnp.where(has_prev, z - 1, z + 1)

    def next_copy(j):
        return remote(
            kvw.at[rows(OWN + j * BLOCK), :], kvw.at[rows(CHUNK + j * BLOCK), :],
            f_s.at[j], f_r.at[j], (g, above, c),
        )

    def relay_copy(j):
        return remote(
            kvw.at[rows(CHUNK + j * BLOCK), :], kvw.at[rows(j * BLOCK), :],
            g_s.at[j], g_r.at[j], (g, above, c),
        )

    spread_own(*kv_way, 3).wait()

    @pl.when(has_next)
    def _():
        next_copy(c).start()

    def pass_on(k):
        j = lax.rem(c + N_CTX - k, N_CTX)
        spread_in(*kv_way, kv_s, kv_r, j).wait_recv()

        @pl.when(has_next)
        def _():
            next_copy(j).start()

    loop(1, N_CTX, pass_on)
    loop(1, N_CTX, lambda k: spread(*d_way, d_s, d_r, lax.rem(c + k, N_CTX)).start())
    spread_own(*d_way, 5).start()

    @pl.when(is_diag)
    def _():
        loop(1, N_GRP, lambda k: group_copy(lax.rem(g + k, N_GRP), k).wait_recv())
        loop(1, N_ULY, lambda k: column_copy(k).start())

    def tables(j):
        cosine_j, sine_j = cos_sin(start + j * BLOCK, lens)
        cosines[rows(j * BLOCK), :] = cosine_j
        sines[rows(j * BLOCK), :] = sine_j

    loop(0, N_CTX, tables)

    def key_masks(j):
        inside, lane = membership(start + j * BLOCK - OWN, lens, BLOCK)
        aug[rows(j * BLOCK), :] = jnp.where(inside | (lane >= 3), 0.0, neg_fill).astype(bf16)

    loop(0, WIN // BLOCK, key_masks)

    def query_masks(r):
        inside, lane = membership(start + r * TQ, lens, TQ)
        hot = jnp.where(inside & (lane < 3), 1.0, 0.0).astype(bf16)
        for h in range(QH):
            onehot[pl.ds(pl.multiple_of(r * LANES + h * TQ, TQ), TQ), :] = hot

    loop(0, ROW_TILES, query_masks)
    def clear(j):
        dkv[rows(j * BLOCK), :] = jnp.zeros((BLOCK, 256), f32)

    loop(0, WIN // BLOCK, clear)

    def pass_far(k):
        j = lax.rem(k + 4, N_CTX)

        @pl.when(has_prev)
        def _():
            next_copy(j).wait_recv()

        @pl.when(middle)
        def _():
            relay_copy(j).start()

    loop(0, N_CTX, pass_far)
    spread_own(*q_way, 6).wait()

    @pl.when(jnp.logical_not(is_diag))
    def _():
        column_copy(1).wait_recv()

    for n in range(N_GRP):
        kp[32 * n : 32 * n + 32, :] = pb[n, 0:32, :]
        vp[32 * n : 32 * n + 32, :] = pb[n, 32:64, :]

    def keys_at(at, count):
        return pl.ds(pl.multiple_of(at, 256), count)

    def tile_rows(r):
        return pl.ds(pl.multiple_of(r * LANES, LANES), LANES)

    def masked_queries(r):
        return jnp.concatenate([onehot[tile_rows(r), :], qst[tile_rows(r), :]], axis=1)

    def masked_keys(at, count):
        return jnp.concatenate([aug[keys_at(at, count), :], kvw[keys_at(at, count), 0:128]], axis=1)

    def head_keys(r):
        first = jnp.concatenate([jnp.zeros((PROMPT_TOKENS, 128), bf16), kp[...]], axis=1)
        return jnp.concatenate([first, masked_keys(OWN + r * TQ, TQ)], axis=0)

    def head_values(r):
        return jnp.concatenate([vp[...], kvw[keys_at(OWN + r * TQ, TQ), 128:256]], axis=0)

    def head_scores(r, qa):
        s = dot_nt(head_keys(r), qa)
        key = lax.broadcasted_iota(i32, (HEAD_KEYS, LANES), 0) - PROMPT_TOKENS
        token = lax.broadcasted_iota(i32, (HEAD_KEYS, LANES), 1) % TQ
        return jnp.where(key <= token, s, neg_fill)

    head_at = pl.ds(HEAD_AT, HEAD_KEYS)

    def first_step(r):
        return jnp.where(has_far, r // 2, jnp.where(has_prev, CHUNK // STEP, OWN // STEP))

    def forward(k):
        r = ROW_TILES - 1 - k

        for e in range(2):
            j = 2 * r + e

            @pl.when(j != c)
            def _():
                spread_in(*q_way, q_s, q_r, j).wait_recv()

        at_rows = pl.ds(pl.multiple_of(r * TQ, TQ), TQ)
        for h in range(QH):
            to = pl.ds(pl.multiple_of(r * LANES + h * TQ, TQ), TQ)
            qst[to, :] = qx[at_rows, 128 * h : 128 * h + 128]
        qa = masked_queries(r)
        low = first_step(r)

        s = head_scores(r, qa)
        s_all[head_at, :] = s
        top = jnp.max(s, axis=0, keepdims=True)

        def score(at, count, top):
            s = dot_nt(masked_keys(at, count), qa)
            s_all[keys_at(at, count), :] = s
            return jnp.maximum(top, jnp.max(s, axis=0, keepdims=True))

        top = lax.fori_loop(0, r, lambda t, a: score(OWN + t * TQ, TQ, a), top)
        near_low = jnp.where(has_prev, CHUNK // STEP, OWN // STEP)
        near_from = jnp.where(has_prev, 1, OWN // CHUNK)
        top = lax.fori_loop(near_from, OWN // CHUNK, lambda t, a: score(t * CHUNK, CHUNK, a), top)

        @pl.when(has_far & (lax.rem(k, 2) == 0))
        def _():
            loop(0, 4, lambda j: relay_copy(4 - 2 * k + j).wait_recv())

        top = lax.fori_loop(low, near_low, lambda t, a: score(t * STEP, STEP, a), top)
        top = top * C2

        def power(at, total):
            p = jnp.exp2(s_all[at, :] * C2 - top)
            s_all[at, :] = p
            return total + jnp.sum(p, axis=0, keepdims=True)

        total = power(head_at, jnp.zeros((1, LANES), f32))
        total = lax.fori_loop(0, r, lambda t, a: power(keys_at(OWN + t * TQ, TQ), a), total)
        total = lax.fori_loop(low, near_low, lambda t, a: power(keys_at(t * STEP, STEP), a), total)
        total = lax.fori_loop(near_from, OWN // CHUNK, lambda t, a: power(keys_at(t * CHUNK, CHUNK), a), total)
        inverse = 1.0 / total
        o_t[...] = dot_tn(head_values(r), (s_all[head_at, :] * inverse).astype(bf16))

        def gather(at, count):
            half = (s_all[keys_at(at, count), :] * inverse).astype(bf16)
            o_t[...] += dot_tn(kvw[keys_at(at, count), 128:256], half)

        loop(0, r, lambda t: gather(OWN + t * TQ, TQ))
        loop(low, near_low, lambda t: gather(t * STEP, STEP))
        loop(near_from, OWN // CHUNK, lambda t: gather(t * CHUNK, CHUNK))
        for e in range(2):
            j = 2 * r + e

            @pl.when(j != c)
            def _():
                spread_in(*d_way, d_s, d_r, j).wait_recv()

            @pl.when(j == c)
            def _():
                spread_own(*d_way, 5).wait()

        for h in range(QH):
            to = pl.ds(pl.multiple_of(r * LANES + h * TQ, TQ), TQ)
            dost[to, :] = dox[at_rows, 128 * h : 128 * h + 128]
        o = o_t[...].astype(bf16).astype(f32)
        delta = jnp.sum(o * dost[tile_rows(r), :].astype(f32).T, axis=0, keepdims=True)
        stats[r, 0:1, :] = top + jnp.log(total) * LOG2E
        stats[r, 1:2, :] = delta
        o_rows = o.T.astype(bf16)
        for h in range(QH):
            ox[at_rows, 128 * h : 128 * h + 128] = o_rows[TQ * h : TQ * h + TQ, :]
        send_rows(ox, out, o_s, o_r, r, 7)

    def home(src, dst, s, r, width, peer):
        return remote(
            src.at[rows(peer * BLOCK), :], dst.at[:, columns(c, width)], s.at[peer], r.at[c], (g, z, peer)
        )

    def home_in(src, dst, s, r, width, j):
        return remote(
            src.at[rows(j * BLOCK), :], dst.at[:, columns(j, width)], s.at[j], r.at[j], (g, z, j)
        )

    def home_own(src, dst, width, at):
        return pltpu.make_async_copy(src.at[rows(c * BLOCK), :], dst.at[:, columns(c, width)], loc.at[at])

    def send_rows(src, dst, s, rs, r, at):
        for e in range(2):
            j = 2 * r + e

            @pl.when(j != c)
            def _():
                home(src, dst, s, rs, 512, j).start()

            @pl.when(j == c)
            def _():
                home_own(src, dst, 512, at).start()

    loop(0, ROW_TILES, forward)

    def grads(r, s, v):
        p = jnp.exp2(s * C2 - stats[r, 0:1, :])
        dp = dot_nt(v, dost[tile_rows(r), :])
        ds = (p * (dp - stats[r, 1:2, :]) * SCALE).astype(bf16)
        return p.astype(bf16), ds

    def backward(r, at, count):
        s = dot_nt(masked_keys(at, count), masked_queries(r))
        here = keys_at(at, count)
        half, ds = grads(r, s, kvw[here, 128:256])
        dq_all[r] += dot_tn(kvw[here, 0:128], ds)
        dkv[here, 0:128] += dot_nn(ds, qst[tile_rows(r), :])
        dkv[here, 128:256] += dot_nn(half, dost[tile_rows(r), :])

    pkg[...] = jnp.zeros((128, 128), f32)
    pvg[...] = jnp.zeros((128, 128), f32)

    def prompt_rows(r):
        half, ds = grads(r, dot_nt(kp[...], qst[tile_rows(r), :]), vp[...])
        dq_all[r] = dot_tn(kp[...], ds)
        pkg[...] += dot_nn(ds, qst[tile_rows(r), :])
        pvg[...] += dot_nn(half, dost[tile_rows(r), :])

    loop(0, ROW_TILES, prompt_rows)
    for n in range(N_GRP):
        pgb[n, 0:32, :] = pkg[32 * n : 32 * n + 32, :].astype(bf16)
        pgb[n, 32:64, :] = pvg[32 * n : 32 * n + 32, :].astype(bf16)

    def to_hub(at):
        return remote(pgb, pgin.at[at], ga_s.at[0], ga_r.at[at], hub)

    def over_groups(at, k):
        gg = lax.rem(g + k, N_GRP)
        return remote(tot.at[gg], bin.at[at], gb_s.at[k], gb_r.at[at], (gg, z, c))

    def to_owner(k):
        cc = lax.rem(c + k, N_CTX)
        return remote(ft.at[cc], pfin, gc_s.at[k], gc_r.at[0], (g, z, cc))

    @pl.when(is_diag)
    def _():
        pgin[z] = pgb[...]

    @pl.when(jnp.logical_not(is_diag))
    def _():
        to_hub(z).start()

    def far_copy(j):
        return remote(
            far_out.at[rows(j * BLOCK), :], far_in.at[rows(j * BLOCK), :], fo_s.at[j], fo_r.at[j], (g, below, c)
        )

    def near_copy(j):
        return remote(
            near_out.at[rows(j * BLOCK), :], near_in.at[rows(j * BLOCK), :], no_s.at[j], no_r.at[j], (g, below, c)
        )

    def send_far(j):
        far_out[rows(j * BLOCK), :] = dkv[rows(j * BLOCK), :].astype(bf16)
        far_copy(j).start()

    blocks = STEP // BLOCK

    @pl.when(has_far)
    def _():
        def far_keys(t):
            loop(0, 2 + 2 * t, lambda r: backward(r, t * STEP, STEP))
            loop(blocks * t, blocks * t + blocks, send_far)

        loop(0, CHUNK // STEP, far_keys)

    @pl.when(is_diag)
    def _():
        loop(1, N_ULY, lambda k: to_hub(lax.rem(z + k, N_ULY)).wait_recv())
        for n in range(N_GRP):
            part = pgin[0, n].astype(f32)
            for m in range(1, N_ULY):
                part = part + pgin[m, n].astype(f32)
            tot[n] = part
        bin[g] = tot[g]

    def send_near(j):
        mine = dkv[rows(CHUNK + j * BLOCK), :]

        @pl.when(middle)
        def _():
            far_copy(j).wait_recv()
            near_out[rows(j * BLOCK), :] = (mine + far_in[rows(j * BLOCK), :].astype(f32)).astype(bf16)

        @pl.when(jnp.logical_not(middle))
        def _():
            near_out[rows(j * BLOCK), :] = mine.astype(bf16)

        near_copy(j).start()

    @pl.when(has_prev)
    def _():
        def near_keys(t):
            loop(0, ROW_TILES, lambda r: backward(r, CHUNK + t * STEP, STEP))
            loop(blocks * t, blocks * t + blocks, send_near)

        loop(0, CHUNK // STEP, near_keys)

    @pl.when(is_diag)
    def _():
        loop(1, N_GRP, lambda k: over_groups(g, k).start())

    def own_rows(k):
        r = lax.rem(c // 2 + k, ROW_TILES)
        loop(0, r, lambda t: backward(r, OWN + t * TQ, TQ))
        here = keys_at(OWN + r * TQ, TQ)
        s = dot_nt(masked_keys(OWN + r * TQ, TQ), masked_queries(r))
        key = lax.broadcasted_iota(i32, (TQ, LANES), 0)
        token = lax.broadcasted_iota(i32, (TQ, LANES), 1) % TQ
        half, ds = grads(r, jnp.where(key <= token, s, neg_fill), kvw[here, 128:256])
        back = dq_all[r] + dot_tn(kvw[here, 0:128], ds)
        dkv[here, 0:128] += dot_nn(ds, qst[tile_rows(r), :])
        dkv[here, 128:256] += dot_nn(half, dost[tile_rows(r), :])
        tau = start + r * TQ + lax.broadcasted_iota(i32, (1, TQ), 1)
        pos = (PROMPT_TOKENS + tau - begins_of(tau, lens)).astype(f32)
        angle = frequency_of(lax.broadcasted_iota(i32, (64, TQ), 0)) * pos
        cosine_t = jnp.concatenate([jnp.cos(angle)] * QH, axis=1)
        sine_t = jnp.concatenate([jnp.sin(angle)] * QH, axis=1)
        x1, x2 = back[0:64, :], back[64:128, :]
        turned_back = jnp.concatenate([x1 * cosine_t + x2 * sine_t, x2 * cosine_t - x1 * sine_t], axis=0)
        q_rows = turned_back.T.astype(bf16)
        at_rows = pl.ds(pl.multiple_of(r * TQ, TQ), TQ)
        for h in range(QH):
            dqx[at_rows, 128 * h : 128 * h + 128] = q_rows[TQ * h : TQ * h + TQ, :]
        send_rows(dqx, dq, dq_s, dq_r, r, 8)

    loop(0, ROW_TILES, own_rows)

    def finish_block(total, j):
        x = total[:, 0:128]
        cosine_j, sine_j = cosines[rows(j * BLOCK), :], sines[rows(j * BLOCK), :]
        own[0, rows(j * BLOCK), :] = (x * cosine_j - pltpu.roll(x, 64, 1) * sine_j).astype(bf16)
        own[1, rows(j * BLOCK), :] = total[:, 128:256].astype(bf16)

    def send_own(k):
        j = 4 * (k // 4) + lax.rem(c + k, 4)
        mine = dkv[rows(OWN + j * BLOCK), :]

        @pl.when(has_next)
        def _():
            near_copy(j).wait_recv()
            finish_block(mine + near_in[rows(j * BLOCK), :].astype(f32), j)

        @pl.when(jnp.logical_not(has_next))
        def _():
            finish_block(mine, j)

        @pl.when(j != c)
        def _():
            home(own.at[0], dk, k_s, k_r, 128, j).start()
            home(own.at[1], dv, v_s, v_r, 128, j).start()

    loop(0, N_CTX, send_own)
    home_own(own.at[0], dk, 128, 10).start()
    home_own(own.at[1], dv, 128, 11).start()

    @pl.when(is_diag)
    def _():
        loop(1, N_GRP, lambda k: over_groups(lax.rem(g + k, N_GRP), k).wait_recv())
        whole = bin[0] + bin[1] + bin[2] + bin[3]
        for n in range(N_CTX):
            ft[n, 0:4, :] = whole[4 * n : 4 * n + 4, :]
            ft[n, 4:8, :] = whole[32 + 4 * n : 36 + 4 * n, :]
        loop(1, N_CTX, lambda k: to_owner(k).start())
        pfin[...] = ft[c]

    @pl.when(is_diag)
    def _():
        loop(1, N_GRP, lambda k: group_copy(g, k).wait_send())
        loop(1, N_ULY, lambda k: column_copy(k).wait_send())
        loop(1, N_GRP, lambda k: over_groups(g, k).wait_send())
        loop(1, N_CTX, lambda k: to_owner(k).wait_send())

    @pl.when(jnp.logical_not(is_diag))
    def _():
        tile_copy(c).wait_send()
        to_hub(z).wait_send()
        to_owner(1).wait_recv()

    total = pfin[...]
    dpk[...] = total[0:4, :].astype(bf16)
    dpv[...] = total[4:8, :].astype(bf16)

    backs = (
        (ox, out, o_s, o_r, 512),
        (dqx, dq, dq_s, dq_r, 512),
        (own.at[0], dk, k_s, k_r, 128),
        (own.at[1], dv, v_s, v_r, 128),
    )

    def finish(k):
        j = lax.rem(c + k, N_CTX)
        spread(*kv_way, kv_s, kv_r, j).wait_send()
        spread(*d_way, d_s, d_r, j).wait_send()
        spread(*q_way, q_s, q_r, j).wait_send()
        for back in backs:
            home(*back, j).wait_send()
            home_in(*back, j).wait_recv()

    loop(1, N_CTX, finish)
    for at, (src, dst, _, _, width) in zip((7, 8, 10, 11), backs):
        home_own(src, dst, width, at).wait()

    def finish_z(j):
        @pl.when(has_next)
        def _():
            next_copy(j).wait_send()

        @pl.when(middle)
        def _():
            relay_copy(j).wait_send()

        @pl.when(has_far)
        def _():
            far_copy(j).wait_send()

        @pl.when(has_prev)
        def _():
            near_copy(j).wait_send()

    loop(0, N_CTX, finish_z)


def place(*refs):
    sems = refs[-1]
    count = (len(refs) - 1) // 2
    copies = [pltpu.make_async_copy(refs[i], refs[count + i], sems.at[i]) for i in range(count)]
    for copy in copies:
        copy.start()
    for copy in copies:
        copy.wait()


def spec(space):
    return pl.BlockSpec(memory_space=space)


VMEM, SMEM, HBM, ANY = pltpu.VMEM, pltpu.SMEM, pltpu.HBM, pl.ANY
DMA = pltpu.SemaphoreType.DMA


def local(queries, keys_in, values_in, out_grad, lengths, prompt_keys, prompt_values):
    sds = jax.ShapeDtypeStruct
    shapes = (
        sds((BLOCK, 4096), bf16),
        sds((BLOCK, 4096), bf16),
        sds((BLOCK, 1024), bf16),
        sds((BLOCK, 1024), bf16),
        sds((4, 128), bf16),
        sds((4, 128), bf16),
    )
    results = pl.pallas_call(
        step_kernel,
        out_shape=shapes,
        in_specs=[spec(HBM)] * 4 + [spec(SMEM), spec(HBM), spec(HBM)],
        out_specs=(spec(VMEM),) * 6,
        scratch_shapes=[
            VMEM((BLOCK, 4096), bf16),
            VMEM((BLOCK, 1024), bf16),
            VMEM((BLOCK, 1024), bf16),
            VMEM((4, 128), bf16),
            VMEM((4, 128), bf16),
            VMEM((BLOCK, 4096), bf16),
            VMEM((BLOCK, 2048), bf16),
            VMEM((8, 128), f32),
            VMEM((N_CTX, 8, 128), f32),
            VMEM((64, 128), f32),
            VMEM((N_GRP, 64, 128), bf16),
            VMEM((CHUNK, 512), bf16),
            VMEM((CHUNK, 512), bf16),
            VMEM((WIN, 256), bf16),
            VMEM((WIN, 128), bf16),
            VMEM((ROW_TILES * LANES, 128), bf16),
            VMEM((ROW_TILES * LANES, 128), bf16),
            VMEM((ROW_TILES * LANES, 128), bf16),
            VMEM((128, 128), bf16),
            VMEM((128, 128), bf16),
            VMEM((HEAD_AT + HEAD_KEYS, LANES), f32),
            VMEM((128, LANES), f32),
            VMEM((ROW_TILES, 128, LANES), f32),
            VMEM((ROW_TILES, 8, LANES), f32),
            VMEM((WIN, 256), f32),
            VMEM((128, 128), f32),
            VMEM((128, 128), f32),
            VMEM((N_GRP, 64, 128), bf16),
            VMEM((N_ULY, N_GRP, 64, 128), bf16),
            VMEM((N_GRP, 64, 128), f32),
            VMEM((N_GRP, 64, 128), f32),
            VMEM((N_CTX, 8, 128), f32),
            VMEM((8, 128), f32),
            VMEM((CHUNK, 512), bf16),
            VMEM((CHUNK, 512), bf16),
        ]
        + [VMEM((CHUNK, 256), bf16)] * 4
        + [VMEM((2, CHUNK, 128), bf16), VMEM((CHUNK, 128), f32), VMEM((CHUNK, 128), f32)]
        + [DMA((8,))] * 22
        + [DMA((8,))] * 12
        + [DMA((14,))],
        compiler_params=pltpu.CompilerParams(
            collective_id=0, has_side_effects=True, vmem_limit_bytes=56 << 20
        ),
        name="grpo_step",
    )(queries, out_grad, keys_in, values_in, lengths[0], prompt_keys, prompt_values)
    return pl.pallas_call(
        place,
        out_shape=shapes,
        in_specs=[spec(VMEM)] * 6,
        out_specs=(spec(HBM),) * 6,
        scratch_shapes=[DMA((6,))],
        name="place",
    )(*results)


def solution(mesh):
    tokens = P(("grp", "uly", "ctx"), None)
    prompt = P(("grp", "ctx"), "uly")
    in_specs = (tokens, tokens, tokens, tokens, P("grp", None, None), prompt, prompt)
    out_specs = (tokens, tokens, tokens, tokens, prompt, prompt)
    return jax.shard_map(local, mesh=mesh, in_specs=in_specs, out_specs=out_specs, check_vma=False)
```

```python
import jax
import jax.numpy as jnp
from jax import lax
from jax.experimental import pallas as pl
from jax.experimental.pallas import tpu as pltpu
from jax.sharding import PartitionSpec as P

H = 32
KEY_VALUE_HEADS = 8
HEAD_WIDTH = 128
PROMPT_TOKENS = 128
theta_base = 1000000.0
neg_fill = -1e30

N_GRP, N_ULY, N_CTX = 4, 8, 8
BLOCK = 128
CHUNK = N_CTX * BLOCK
RUN_PLACES = 4
QH = H // KEY_VALUE_HEADS
WIN = 3 * CHUNK
OWN = 2 * CHUNK
TQ = 256
ROW_TILES = CHUNK // TQ
LANES = QH * TQ
STEP = 512
HEAD_KEYS = PROMPT_TOKENS + TQ
HEAD_AT = WIN - TQ
SCALE = HEAD_WIDTH**-0.5
LOG2E = 1.4426950408889634
C2 = SCALE * LOG2E
MESH = pl.DeviceIdType.MESH
f32, bf16, i32 = jnp.float32, jnp.bfloat16, jnp.int32


def frequency_of(index):
    out = jnp.ones(index.shape, f32)
    for bit in range(6):
        power = theta_base ** (-(2.0 * 2**bit) / HEAD_WIDTH)
        out = out * jnp.where((index // 2**bit) % 2 == 1, f32(power), f32(1.0))
    return out


def begins_of(tau, lens):
    l0, l1, l2 = lens
    zero = jnp.zeros_like(tau)
    return (
        jnp.where(tau >= l0, l0, zero)
        + jnp.where(tau >= l0 + l1, l1, zero)
        + jnp.where(tau >= l0 + l1 + l2, l2, zero)
    )


def cos_sin(base, lens):
    tau = base + lax.broadcasted_iota(i32, (BLOCK, HEAD_WIDTH), 0)
    pos = PROMPT_TOKENS + tau - begins_of(tau, lens)
    lane = lax.broadcasted_iota(i32, (BLOCK, HEAD_WIDTH), 1)
    freq = frequency_of(lax.broadcasted_iota(i32, (8, HEAD_WIDTH), 1) % 64)[0:1, :]
    angle = pos.astype(f32) * freq
    sine = jnp.sin(angle)
    return jnp.cos(angle), jnp.where(lane < 64, -sine, sine)


def membership(base, lens, count):
    l0, l1, l2 = lens
    tau = base + lax.broadcasted_iota(i32, (count, HEAD_WIDTH), 0)
    lane = lax.broadcasted_iota(i32, (count, HEAD_WIDTH), 1)
    low = jnp.where(lane == 0, 0, jnp.where(lane == 1, l0, l0 + l1))
    high = jnp.where(lane == 0, l0, jnp.where(lane == 1, l0 + l1, l0 + l1 + l2))
    return (tau >= low) & (tau < high), lane


def dot_nt(a, b):
    return lax.dot_general(a, b, (((1,), (1,)), ((), ())), preferred_element_type=f32)


def dot_nn(a, b):
    return lax.dot_general(a, b, (((1,), (0,)), ((), ())), preferred_element_type=f32)


def dot_tn(a, b):
    return lax.dot_general(a, b, (((0,), (0,)), ((), ())), preferred_element_type=f32)


def step_kernel(
    q_hbm, do_hbm, k_hbm, v_hbm, len_ref, pk_hbm, pv_hbm,
    out, dq, dk, dv, dpk, dpv,
    q_in, k_in, v_in, pk_in, pv_in, qrot, kvs, ptile, pta, rows64, pb, qx, dox, kvw, aug, onehot, qst, dost, kp, vp,
    s_all, o_t, dq_all, stats, dkv, pkg, pvg, pgb, pgin, tot, bin, ft, pfin, ox, dqx,
    far_out, far_in, near_out, near_in, own, cosines, sines,
    q_s, q_r, d_s, d_r, kv_s, kv_r, f_s, f_r, g_s, g_r, o_s, o_r, dq_s, dq_r,
    fo_s, fo_r, no_s, no_r, k_s, k_r, v_s, v_r, p_s, p_r, pb_s, pb_r, pc_s, pc_r, ga_s, ga_r, gb_s, gb_r, gc_s, gc_r, loc,
):
    g, z, c = lax.axis_index("grp"), lax.axis_index("uly"), lax.axis_index("ctx")
    zr = lax.rem(z, RUN_PLACES)
    run = z // RUN_PLACES
    start = zr * CHUNK
    has_next, has_prev = zr < RUN_PLACES - 1, zr > 0
    middle = (zr == 1) | (zr == 2)
    has_far = zr >= 2
    is_diag = z == c
    lens = (len_ref[run, 0], len_ref[run, 1], len_ref[run, 2])
    barrier = pltpu.get_barrier_semaphore()

    def loop(low, high, body):
        def run_body(i, _):
            body(i)
            return 0

        lax.fori_loop(low, high, run_body, 0)

    def rows(at):
        return pl.ds(pl.multiple_of(at, BLOCK), BLOCK)

    def columns(at, width):
        return pl.ds(pl.multiple_of(at * width, width), width)

    def remote(src, dst, s, r, dev):
        return pltpu.make_async_remote_copy(
            src_ref=src, dst_ref=dst, send_sem=s, recv_sem=r, device_id=dev, device_id_type=MESH
        )

    load_k = pltpu.make_async_copy(k_hbm, k_in, loc.at[0])
    load_v = pltpu.make_async_copy(v_hbm, v_in, loc.at[1])
    load_q = pltpu.make_async_copy(q_hbm, q_in, loc.at[2])
    load_k.start()
    load_v.start()
    load_q.start()
    load_pk = pltpu.make_async_copy(pk_hbm, pk_in, loc.at[12])
    load_pv = pltpu.make_async_copy(pv_hbm, pv_in, loc.at[13])
    load_pk.start()
    load_pv.start()

    def greet(dev):
        pl.semaphore_signal(barrier, inc=1, device_id=dev, device_id_type=MESH)

    loop(1, N_CTX, lambda k: greet((g, z, lax.rem(c + k, N_CTX))))

    @pl.when(has_prev)
    def _():
        greet((g, z - 1, c))

    @pl.when(has_next)
    def _():
        greet((g, z + 1, c))

    hub = (g, c, c)

    @pl.when(is_diag)
    def _():
        loop(1, N_ULY, lambda k: greet((g, lax.rem(z + k, N_ULY), c)))
        loop(1, N_GRP, lambda k: greet((lax.rem(g + k, N_GRP), z, c)))

    @pl.when(jnp.logical_not(is_diag))
    def _():
        greet(hub)

    cosine, sine = cos_sin(start + c * BLOCK, lens)

    def turned(block):
        x = block.astype(f32)
        return (x * cosine + pltpu.roll(x, 64, 1) * sine).astype(bf16)

    load_k.wait()
    load_v.wait()
    for j in range(KEY_VALUE_HEADS):
        kvs[:, 256 * j : 256 * j + 128] = turned(k_in[:, 128 * j : 128 * j + 128])
        kvs[:, 256 * j + 128 : 256 * j + 256] = v_in[:, 128 * j : 128 * j + 128]
    load_pk.wait()
    load_pv.wait()
    ptile[0:4, :] = pk_in[...].astype(f32)
    ptile[4:8, :] = pv_in[...].astype(f32)

    pl.semaphore_wait(
        barrier,
        (N_CTX - 1)
        + jnp.where(has_next, 1, 0)
        + jnp.where(has_prev, 1, 0)
        + jnp.where(is_diag, N_ULY - 1 + N_GRP - 1, 1),
    )

    def spread(src, width, dst, base, s, r, peer):
        return remote(
            src.at[:, columns(peer, width)], dst.at[rows(base + c * BLOCK), :],
            s.at[peer], r.at[c], (g, z, peer),
        )

    def spread_in(src, width, dst, base, s, r, j):
        return remote(
            src.at[:, columns(j, width)], dst.at[rows(base + j * BLOCK), :], s.at[j], r.at[j], (g, z, j)
        )

    def spread_own(src, width, dst, base, at):
        return pltpu.make_async_copy(
            src.at[:, columns(c, width)], dst.at[rows(base + c * BLOCK), :], loc.at[at]
        )

    kv_way = (kvs, 256, kvw, OWN)
    d_way = (do_hbm, 512, dox, 0)
    q_way = (qrot, 512, qx, 0)
    loop(1, N_CTX, lambda k: spread(*kv_way, kv_s, kv_r, lax.rem(c + k, N_CTX)).start())
    spread_own(*kv_way, 3).start()

    def tile_copy(at):
        return remote(ptile, pta.at[at], p_s.at[0], p_r.at[at], (g, z, z))

    def group_copy(at, k):
        return remote(pb.at[at], pb.at[at], pb_s.at[k], pb_r.at[at], (lax.rem(g + k, N_GRP), z, c))

    def column_copy(k):
        return remote(pb, pb, pc_s.at[k], pc_r.at[0], (g, lax.rem(z + k, N_ULY), c))

    @pl.when(is_diag)
    def _():
        pta[c] = ptile[...]

    @pl.when(jnp.logical_not(is_diag))
    def _():
        tile_copy(c).start()

    load_q.wait()

    def turn_heads(peer):
        for h in range(QH):
            at = columns(peer * QH + h, 128)
            qrot[:, at] = turned(q_in[:, at])

    def start_q(k):
        peer = lax.rem(c + k, N_CTX)
        turn_heads(peer)
        spread(*q_way, q_s, q_r, peer).start()

    loop(1, N_CTX, start_q)
    turn_heads(c)
    spread_own(*q_way, 6).start()

    @pl.when(is_diag)
    def _():
        loop(1, N_CTX, lambda k: tile_copy(lax.rem(c + k, N_CTX)).wait_recv())
        for n in range(N_CTX):
            rows64[4 * n : 4 * n + 4, :] = pta[n, 0:4, :]
            rows64[32 + 4 * n : 36 + 4 * n, :] = pta[n, 4:8, :]
        pb[g] = rows64[...].astype(bf16)
        loop(1, N_GRP, lambda k: group_copy(g, k).start())

    above = jnp.where(has_next, z + 1, z - 1)
    below = jnp.where(has_prev, z - 1, z + 1)

    def next_copy(j):
        return remote(
            kvw.at[rows(OWN + j * BLOCK), :], kvw.at[rows(CHUNK + j * BLOCK), :],
            f_s.at[j], f_r.at[j], (g, above, c),
        )

    def relay_copy(j):
        return remote(
            kvw.at[rows(CHUNK + j * BLOCK), :], kvw.at[rows(j * BLOCK), :],
            g_s.at[j], g_r.at[j], (g, above, c),
        )

    spread_own(*kv_way, 3).wait()

    @pl.when(has_next)
    def _():
        next_copy(c).start()

    def pass_on(k):
        j = lax.rem(c + N_CTX - k, N_CTX)
        spread_in(*kv_way, kv_s, kv_r, j).wait_recv()

        @pl.when(has_next)
        def _():
            next_copy(j).start()

    loop(1, N_CTX, pass_on)
    loop(1, N_CTX, lambda k: spread(*d_way, d_s, d_r, lax.rem(c + k, N_CTX)).start())
    spread_own(*d_way, 5).start()

    @pl.when(is_diag)
    def _():
        loop(1, N_GRP, lambda k: group_copy(lax.rem(g + k, N_GRP), k).wait_recv())
        loop(1, N_ULY, lambda k: column_copy(k).start())

    def tables(j):
        cosine_j, sine_j = cos_sin(start + j * BLOCK, lens)
        cosines[rows(j * BLOCK), :] = cosine_j
        sines[rows(j * BLOCK), :] = sine_j

    loop(0, N_CTX, tables)

    def key_masks(j):
        inside, lane = membership(start + j * BLOCK - OWN, lens, BLOCK)
        aug[rows(j * BLOCK), :] = jnp.where(inside | (lane >= 3), 0.0, neg_fill).astype(bf16)

    loop(0, WIN // BLOCK, key_masks)

    def query_masks(r):
        inside, lane = membership(start + r * TQ, lens, TQ)
        hot = jnp.where(inside & (lane < 3), 1.0, 0.0).astype(bf16)
        for h in range(QH):
            onehot[pl.ds(pl.multiple_of(r * LANES + h * TQ, TQ), TQ), :] = hot

    loop(0, ROW_TILES, query_masks)
    def clear(j):
        dkv[rows(j * BLOCK), :] = jnp.zeros((BLOCK, 256), f32)

    loop(0, WIN // BLOCK, clear)

    def pass_far(k):
        j = lax.rem(k + 4, N_CTX)

        @pl.when(has_prev)
        def _():
            next_copy(j).wait_recv()

        @pl.when(middle)
        def _():
            relay_copy(j).start()

    loop(0, N_CTX, pass_far)
    spread_own(*q_way, 6).wait()

    def keys_at(at, count):
        return pl.ds(pl.multiple_of(at, 256), count)

    def tile_rows(r):
        return pl.ds(pl.multiple_of(r * LANES, LANES), LANES)

    def masked_queries(r):
        return jnp.concatenate([onehot[tile_rows(r), :], qst[tile_rows(r), :]], axis=1)

    def masked_keys(at, count):
        return jnp.concatenate([aug[keys_at(at, count), :], kvw[keys_at(at, count), 0:128]], axis=1)

    def head_keys(r):
        first = jnp.concatenate([jnp.zeros((PROMPT_TOKENS, 128), bf16), kp[...]], axis=1)
        return jnp.concatenate([first, masked_keys(OWN + r * TQ, TQ)], axis=0)

    def head_values(r):
        return jnp.concatenate([vp[...], kvw[keys_at(OWN + r * TQ, TQ), 128:256]], axis=0)

    def head_scores(r, qa):
        s = dot_nt(head_keys(r), qa)
        key = lax.broadcasted_iota(i32, (HEAD_KEYS, LANES), 0) - PROMPT_TOKENS
        token = lax.broadcasted_iota(i32, (HEAD_KEYS, LANES), 1) % TQ
        return jnp.where(key <= token, s, neg_fill)

    head_at = pl.ds(HEAD_AT, HEAD_KEYS)

    def first_step(r):
        return jnp.where(has_far, r // 2, jnp.where(has_prev, CHUNK // STEP, OWN // STEP))

    def take_prompt():
        @pl.when(jnp.logical_not(is_diag))
        def _():
            column_copy(1).wait_recv()

        for n in range(N_GRP):
            kp[32 * n : 32 * n + 32, :] = pb[n, 0:32, :]
            vp[32 * n : 32 * n + 32, :] = pb[n, 32:64, :]

    def forward(k):
        r = ROW_TILES - 1 - k

        for e in range(2):
            j = 2 * r + e

            @pl.when(j != c)
            def _():
                spread_in(*q_way, q_s, q_r, j).wait_recv()

        at_rows = pl.ds(pl.multiple_of(r * TQ, TQ), TQ)
        for h in range(QH):
            to = pl.ds(pl.multiple_of(r * LANES + h * TQ, TQ), TQ)
            qst[to, :] = qx[at_rows, 128 * h : 128 * h + 128]
        qa = masked_queries(r)
        low = first_step(r)

        top = jnp.full((1, LANES), neg_fill, f32)

        def score(at, count, top):
            s = dot_nt(masked_keys(at, count), qa)
            s_all[keys_at(at, count), :] = s
            return jnp.maximum(top, jnp.max(s, axis=0, keepdims=True))

        top = lax.fori_loop(0, r, lambda t, a: score(OWN + t * TQ, TQ, a), top)
        near_low = jnp.where(has_prev, CHUNK // STEP, OWN // STEP)
        near_from = jnp.where(has_prev, 1, OWN // CHUNK)
        top = lax.fori_loop(near_from, OWN // CHUNK, lambda t, a: score(t * CHUNK, CHUNK, a), top)

        @pl.when(has_far & (lax.rem(k, 2) == 0))
        def _():
            loop(0, 4, lambda j: relay_copy(4 - 2 * k + j).wait_recv())

        top = lax.fori_loop(low, near_low, lambda t, a: score(t * STEP, STEP, a), top)

        @pl.when(k == 0)
        def _():
            take_prompt()

        s = head_scores(r, qa)
        s_all[head_at, :] = s
        top = jnp.maximum(top, jnp.max(s, axis=0, keepdims=True))
        top = top * C2

        def power(at, total):
            p = jnp.exp2(s_all[at, :] * C2 - top)
            s_all[at, :] = p
            return total + jnp.sum(p, axis=0, keepdims=True)

        total = power(head_at, jnp.zeros((1, LANES), f32))
        total = lax.fori_loop(0, r, lambda t, a: power(keys_at(OWN + t * TQ, TQ), a), total)
        total = lax.fori_loop(low, near_low, lambda t, a: power(keys_at(t * STEP, STEP), a), total)
        total = lax.fori_loop(near_from, OWN // CHUNK, lambda t, a: power(keys_at(t * CHUNK, CHUNK), a), total)
        inverse = 1.0 / total
        o_t[...] = dot_tn(head_values(r), (s_all[head_at, :] * inverse).astype(bf16))

        def gather(at, count):
            half = (s_all[keys_at(at, count), :] * inverse).astype(bf16)
            o_t[...] += dot_tn(kvw[keys_at(at, count), 128:256], half)

        loop(0, r, lambda t: gather(OWN + t * TQ, TQ))
        loop(low, near_low, lambda t: gather(t * STEP, STEP))
        loop(near_from, OWN // CHUNK, lambda t: gather(t * CHUNK, CHUNK))
        for e in range(2):
            j = 2 * r + e

            @pl.when(j != c)
            def _():
                spread_in(*d_way, d_s, d_r, j).wait_recv()

            @pl.when(j == c)
            def _():
                spread_own(*d_way, 5).wait()

        for h in range(QH):
            to = pl.ds(pl.multiple_of(r * LANES + h * TQ, TQ), TQ)
            dost[to, :] = dox[at_rows, 128 * h : 128 * h + 128]
        o = o_t[...].astype(bf16).astype(f32)
        delta = jnp.sum(o * dost[tile_rows(r), :].astype(f32).T, axis=0, keepdims=True)
        stats[r, 0:1, :] = top + jnp.log(total) * LOG2E
        stats[r, 1:2, :] = delta
        o_rows = o.T.astype(bf16)
        for h in range(QH):
            ox[at_rows, 128 * h : 128 * h + 128] = o_rows[TQ * h : TQ * h + TQ, :]
        send_rows(ox, out, o_s, o_r, r, 7)

    def home(src, dst, s, r, width, peer):
        return remote(
            src.at[rows(peer * BLOCK), :], dst.at[:, columns(c, width)], s.at[peer], r.at[c], (g, z, peer)
        )

    def home_in(src, dst, s, r, width, j):
        return remote(
            src.at[rows(j * BLOCK), :], dst.at[:, columns(j, width)], s.at[j], r.at[j], (g, z, j)
        )

    def home_own(src, dst, width, at):
        return pltpu.make_async_copy(src.at[rows(c * BLOCK), :], dst.at[:, columns(c, width)], loc.at[at])

    def send_rows(src, dst, s, rs, r, at):
        for e in range(2):
            j = 2 * r + e

            @pl.when(j != c)
            def _():
                home(src, dst, s, rs, 512, j).start()

            @pl.when(j == c)
            def _():
                home_own(src, dst, 512, at).start()

    loop(0, ROW_TILES, forward)

    def grads(r, s, v):
        p = jnp.exp2(s * C2 - stats[r, 0:1, :])
        dp = dot_nt(v, dost[tile_rows(r), :])
        ds = (p * (dp - stats[r, 1:2, :]) * SCALE).astype(bf16)
        return p.astype(bf16), ds

    def backward(r, at, count):
        s = dot_nt(masked_keys(at, count), masked_queries(r))
        here = keys_at(at, count)
        half, ds = grads(r, s, kvw[here, 128:256])
        dq_all[r] += dot_tn(kvw[here, 0:128], ds)
        dkv[here, 0:128] += dot_nn(ds, qst[tile_rows(r), :])
        dkv[here, 128:256] += dot_nn(half, dost[tile_rows(r), :])

    pkg[...] = jnp.zeros((128, 128), f32)
    pvg[...] = jnp.zeros((128, 128), f32)

    def prompt_rows(r):
        half, ds = grads(r, dot_nt(kp[...], qst[tile_rows(r), :]), vp[...])
        dq_all[r] = dot_tn(kp[...], ds)
        pkg[...] += dot_nn(ds, qst[tile_rows(r), :])
        pvg[...] += dot_nn(half, dost[tile_rows(r), :])

    loop(0, ROW_TILES, prompt_rows)
    for n in range(N_GRP):
        pgb[n, 0:32, :] = pkg[32 * n : 32 * n + 32, :].astype(bf16)
        pgb[n, 32:64, :] = pvg[32 * n : 32 * n + 32, :].astype(bf16)

    def to_hub(at):
        return remote(pgb, pgin.at[at], ga_s.at[0], ga_r.at[at], hub)

    def over_groups(at, k):
        gg = lax.rem(g + k, N_GRP)
        return remote(tot.at[gg], bin.at[at], gb_s.at[k], gb_r.at[at], (gg, z, c))

    def to_owner(k):
        cc = lax.rem(c + k, N_CTX)
        return remote(ft.at[cc], pfin, gc_s.at[k], gc_r.at[0], (g, z, cc))

    @pl.when(is_diag)
    def _():
        pgin[z] = pgb[...]

    @pl.when(jnp.logical_not(is_diag))
    def _():
        to_hub(z).start()

    def far_copy(j):
        return remote(
            far_out.at[rows(j * BLOCK), :], far_in.at[rows(j * BLOCK), :], fo_s.at[j], fo_r.at[j], (g, below, c)
        )

    def near_copy(j):
        return remote(
            near_out.at[rows(j * BLOCK), :], near_in.at[rows(j * BLOCK), :], no_s.at[j], no_r.at[j], (g, below, c)
        )

    def send_far(j):
        far_out[rows(j * BLOCK), :] = dkv[rows(j * BLOCK), :].astype(bf16)
        far_copy(j).start()

    blocks = STEP // BLOCK

    @pl.when(has_far)
    def _():
        def far_keys(t):
            loop(0, 2 + 2 * t, lambda r: backward(r, t * STEP, STEP))
            loop(blocks * t, blocks * t + blocks, send_far)

        loop(0, CHUNK // STEP, far_keys)

    @pl.when(is_diag)
    def _():
        loop(1, N_ULY, lambda k: to_hub(lax.rem(z + k, N_ULY)).wait_recv())
        for n in range(N_GRP):
            part = pgin[0, n].astype(f32)
            for m in range(1, N_ULY):
                part = part + pgin[m, n].astype(f32)
            tot[n] = part
        bin[g] = tot[g]

    def send_near(j):
        mine = dkv[rows(CHUNK + j * BLOCK), :]

        @pl.when(middle)
        def _():
            far_copy(j).wait_recv()
            near_out[rows(j * BLOCK), :] = (mine + far_in[rows(j * BLOCK), :].astype(f32)).astype(bf16)

        @pl.when(jnp.logical_not(middle))
        def _():
            near_out[rows(j * BLOCK), :] = mine.astype(bf16)

        near_copy(j).start()

    @pl.when(has_prev)
    def _():
        def near_keys(t):
            loop(0, ROW_TILES, lambda r: backward(r, CHUNK + t * STEP, STEP))
            loop(blocks * t, blocks * t + blocks, send_near)

        loop(0, CHUNK // STEP, near_keys)

    @pl.when(is_diag)
    def _():
        loop(1, N_GRP, lambda k: over_groups(g, k).start())

    def own_rows(k):
        r = lax.rem(c // 2 + k, ROW_TILES)
        loop(0, r, lambda t: backward(r, OWN + t * TQ, TQ))
        here = keys_at(OWN + r * TQ, TQ)
        s = dot_nt(masked_keys(OWN + r * TQ, TQ), masked_queries(r))
        key = lax.broadcasted_iota(i32, (TQ, LANES), 0)
        token = lax.broadcasted_iota(i32, (TQ, LANES), 1) % TQ
        half, ds = grads(r, jnp.where(key <= token, s, neg_fill), kvw[here, 128:256])
        back = dq_all[r] + dot_tn(kvw[here, 0:128], ds)
        dkv[here, 0:128] += dot_nn(ds, qst[tile_rows(r), :])
        dkv[here, 128:256] += dot_nn(half, dost[tile_rows(r), :])
        tau = start + r * TQ + lax.broadcasted_iota(i32, (1, TQ), 1)
        pos = (PROMPT_TOKENS + tau - begins_of(tau, lens)).astype(f32)
        angle = frequency_of(lax.broadcasted_iota(i32, (64, TQ), 0)) * pos
        cosine_t = jnp.concatenate([jnp.cos(angle)] * QH, axis=1)
        sine_t = jnp.concatenate([jnp.sin(angle)] * QH, axis=1)
        x1, x2 = back[0:64, :], back[64:128, :]
        turned_back = jnp.concatenate([x1 * cosine_t + x2 * sine_t, x2 * cosine_t - x1 * sine_t], axis=0)
        q_rows = turned_back.T.astype(bf16)
        at_rows = pl.ds(pl.multiple_of(r * TQ, TQ), TQ)
        for h in range(QH):
            dqx[at_rows, 128 * h : 128 * h + 128] = q_rows[TQ * h : TQ * h + TQ, :]
        send_rows(dqx, dq, dq_s, dq_r, r, 8)

    loop(0, ROW_TILES, own_rows)

    def finish_block(total, j):
        x = total[:, 0:128]
        cosine_j, sine_j = cosines[rows(j * BLOCK), :], sines[rows(j * BLOCK), :]
        own[0, rows(j * BLOCK), :] = (x * cosine_j - pltpu.roll(x, 64, 1) * sine_j).astype(bf16)
        own[1, rows(j * BLOCK), :] = total[:, 128:256].astype(bf16)

    def send_own(k):
        j = 4 * (k // 4) + lax.rem(c + k, 4)
        mine = dkv[rows(OWN + j * BLOCK), :]

        @pl.when(has_next)
        def _():
            near_copy(j).wait_recv()
            finish_block(mine + near_in[rows(j * BLOCK), :].astype(f32), j)

        @pl.when(jnp.logical_not(has_next))
        def _():
            finish_block(mine, j)

        @pl.when(j != c)
        def _():
            home(own.at[0], dk, k_s, k_r, 128, j).start()
            home(own.at[1], dv, v_s, v_r, 128, j).start()

    loop(0, N_CTX, send_own)
    home_own(own.at[0], dk, 128, 10).start()
    home_own(own.at[1], dv, 128, 11).start()

    @pl.when(is_diag)
    def _():
        loop(1, N_GRP, lambda k: over_groups(lax.rem(g + k, N_GRP), k).wait_recv())
        whole = bin[0] + bin[1] + bin[2] + bin[3]
        for n in range(N_CTX):
            ft[n, 0:4, :] = whole[4 * n : 4 * n + 4, :]
            ft[n, 4:8, :] = whole[32 + 4 * n : 36 + 4 * n, :]
        loop(1, N_CTX, lambda k: to_owner(k).start())
        pfin[...] = ft[c]

    @pl.when(is_diag)
    def _():
        loop(1, N_GRP, lambda k: group_copy(g, k).wait_send())
        loop(1, N_ULY, lambda k: column_copy(k).wait_send())
        loop(1, N_GRP, lambda k: over_groups(g, k).wait_send())
        loop(1, N_CTX, lambda k: to_owner(k).wait_send())

    @pl.when(jnp.logical_not(is_diag))
    def _():
        tile_copy(c).wait_send()
        to_hub(z).wait_send()
        to_owner(1).wait_recv()

    total = pfin[...]
    dpk[...] = total[0:4, :].astype(bf16)
    dpv[...] = total[4:8, :].astype(bf16)

    backs = (
        (ox, out, o_s, o_r, 512),
        (dqx, dq, dq_s, dq_r, 512),
        (own.at[0], dk, k_s, k_r, 128),
        (own.at[1], dv, v_s, v_r, 128),
    )

    def finish(k):
        j = lax.rem(c + k, N_CTX)
        spread(*kv_way, kv_s, kv_r, j).wait_send()
        spread(*d_way, d_s, d_r, j).wait_send()
        spread(*q_way, q_s, q_r, j).wait_send()
        for back in backs:
            home(*back, j).wait_send()
            home_in(*back, j).wait_recv()

    loop(1, N_CTX, finish)
    for at, (src, dst, _, _, width) in zip((7, 8, 10, 11), backs):
        home_own(src, dst, width, at).wait()

    def finish_z(j):
        @pl.when(has_next)
        def _():
            next_copy(j).wait_send()

        @pl.when(middle)
        def _():
            relay_copy(j).wait_send()

        @pl.when(has_far)
        def _():
            far_copy(j).wait_send()

        @pl.when(has_prev)
        def _():
            near_copy(j).wait_send()

    loop(0, N_CTX, finish_z)


def place(*refs):
    sems = refs[-1]
    count = (len(refs) - 1) // 2
    copies = [pltpu.make_async_copy(refs[i], refs[count + i], sems.at[i]) for i in range(count)]
    for copy in copies:
        copy.start()
    for copy in copies:
        copy.wait()


def spec(space):
    return pl.BlockSpec(memory_space=space)


VMEM, SMEM, HBM, ANY = pltpu.VMEM, pltpu.SMEM, pltpu.HBM, pl.ANY
DMA = pltpu.SemaphoreType.DMA


def local(queries, keys_in, values_in, out_grad, lengths, prompt_keys, prompt_values):
    sds = jax.ShapeDtypeStruct
    shapes = (
        sds((BLOCK, 4096), bf16),
        sds((BLOCK, 4096), bf16),
        sds((BLOCK, 1024), bf16),
        sds((BLOCK, 1024), bf16),
        sds((4, 128), bf16),
        sds((4, 128), bf16),
    )
    results = pl.pallas_call(
        step_kernel,
        out_shape=shapes,
        in_specs=[spec(HBM)] * 4 + [spec(SMEM), spec(HBM), spec(HBM)],
        out_specs=(spec(VMEM),) * 6,
        scratch_shapes=[
            VMEM((BLOCK, 4096), bf16),
            VMEM((BLOCK, 1024), bf16),
            VMEM((BLOCK, 1024), bf16),
            VMEM((4, 128), bf16),
            VMEM((4, 128), bf16),
            VMEM((BLOCK, 4096), bf16),
            VMEM((BLOCK, 2048), bf16),
            VMEM((8, 128), f32),
            VMEM((N_CTX, 8, 128), f32),
            VMEM((64, 128), f32),
            VMEM((N_GRP, 64, 128), bf16),
            VMEM((CHUNK, 512), bf16),
            VMEM((CHUNK, 512), bf16),
            VMEM((WIN, 256), bf16),
            VMEM((WIN, 128), bf16),
            VMEM((ROW_TILES * LANES, 128), bf16),
            VMEM((ROW_TILES * LANES, 128), bf16),
            VMEM((ROW_TILES * LANES, 128), bf16),
            VMEM((128, 128), bf16),
            VMEM((128, 128), bf16),
            VMEM((HEAD_AT + HEAD_KEYS, LANES), f32),
            VMEM((128, LANES), f32),
            VMEM((ROW_TILES, 128, LANES), f32),
            VMEM((ROW_TILES, 8, LANES), f32),
            VMEM((WIN, 256), f32),
            VMEM((128, 128), f32),
            VMEM((128, 128), f32),
            VMEM((N_GRP, 64, 128), bf16),
            VMEM((N_ULY, N_GRP, 64, 128), bf16),
            VMEM((N_GRP, 64, 128), f32),
            VMEM((N_GRP, 64, 128), f32),
            VMEM((N_CTX, 8, 128), f32),
            VMEM((8, 128), f32),
            VMEM((CHUNK, 512), bf16),
            VMEM((CHUNK, 512), bf16),
        ]
        + [VMEM((CHUNK, 256), bf16)] * 4
        + [VMEM((2, CHUNK, 128), bf16), VMEM((CHUNK, 128), f32), VMEM((CHUNK, 128), f32)]
        + [DMA((8,))] * 22
        + [DMA((8,))] * 12
        + [DMA((14,))],
        compiler_params=pltpu.CompilerParams(
            collective_id=0, has_side_effects=True, vmem_limit_bytes=56 << 20
        ),
        name="grpo_step",
    )(queries, out_grad, keys_in, values_in, lengths[0], prompt_keys, prompt_values)
    return pl.pallas_call(
        place,
        out_shape=shapes,
        in_specs=[spec(VMEM)] * 6,
        out_specs=(spec(HBM),) * 6,
        scratch_shapes=[DMA((6,))],
        name="place",
    )(*results)


def solution(mesh):
    tokens = P(("grp", "uly", "ctx"), None)
    prompt = P(("grp", "ctx"), "uly")
    in_specs = (tokens, tokens, tokens, tokens, P("grp", None, None), prompt, prompt)
    out_specs = (tokens, tokens, tokens, tokens, prompt, prompt)
    return jax.shard_map(local, mesh=mesh, in_specs=in_specs, out_specs=out_specs, check_vma=False)
```
